256 devices in a mesh: section: 8 (over y, core), expert: 32 (over x, z).
Axes of the slice: x: 4, y: 4, z: 8, core: 2. Of those that a mesh axis runs over, the one named last changes fastest.
Arguments:
- out_grad: bfloat16 [8, 4096, 7168], P('section', 'expert'), may hold values from -6 to 6
- router_weight: bfloat16 [8, 7168, 8], P('section'), may hold values from -0.25 to 0.25
- down_weight: bfloat16 [8, 8192, 7168], P('section', 'expert'), may hold values from -0.1875 to 0.1875
- hidden_saved: bfloat16 [8, 32, 32, 32, 256], P('section', 'expert'), may hold values from -1.5 to 1.5
- slot_token: int32 [8, 32, 8, 32], P('section', 'expert'), may hold values from 0 to 127, as said below
- slot_count: int32 [8, 32, 8], P('section', 'expert'), may hold values from 8 to 32, as said below
- slot_gate: float32 [8, 32, 8, 32], P('section', 'expert'), may hold values from 0.02 to 1
Outputs:
- down_grad: bfloat16 [8, 8192, 7168], P('section', 'expert')
- hidden_grad: bfloat16 [8, 32, 32, 32, 256], P('section', 'expert')
- passed_grad: bfloat16 [8, 4096, 7168], P('section', 'expert')
The draws below stay inside these ranges and needn't reach their ends.
Inputs may be any that keep to these rules, and one draw needn't show every extreme that they name: `slot_token`: within each block the used slots name distinct tokens; entries at slots from the count onward are ignored. `slot_count`: in every section one expert has 32 used slots in the block of every source device.
All inputs are finite; a program needn't handle non-finite values.
Results may differ from the reference program's by a relative error of at most 0.015.
Values may be sent and summed in bfloat16 or wider, within the bound.
No kernel may reach another device: no remote copies, remote signals or barrier semaphores. Data moves between devices by JAX's collectives and lax.ppermute only.
A program may use at most 128 MiB of HBM per device.

```python
import math
import jax
import jax.numpy as jnp
from jax import lax

D = 7168
HID = 1024
GROUP = 4
TOK_DEV = 128
HID_DEV = 256
EXPERTS = 8
CAP = 32
TOKENS = 4096
N_SECTION = 8
N_EXPERT = 32


def draw_slot_token(key, part):
    inner = jax.random.fold_in(key, 11)
    keys = jax.random.split(inner, N_SECTION * N_EXPERT * EXPERTS)
    perms = jax.vmap(lambda k: jax.random.permutation(k, TOK_DEV))(keys)
    return perms[:, :CAP].reshape(N_SECTION, N_EXPERT, EXPERTS, CAP).astype(jnp.int32)


def draw_slot_count(key, part):
    inner = jax.random.fold_in(key, 23)
    first, second = jax.random.split(inner)
    counts = jax.random.randint(first, (N_SECTION, N_EXPERT, EXPERTS), CAP // 4, CAP + 1)
    hottest = jax.random.randint(second, (N_SECTION,), 0, EXPERTS)
    column = lax.broadcasted_iota(jnp.int32, (N_SECTION, N_EXPERT, EXPERTS), 2)
    return jnp.where(column == hottest[:, None, None], CAP, counts).astype(jnp.int32)


def steps_of(key, extent, shards, low, top_value):
    level = 1.0
    for dim, blocks in shards:
        steps = jax.random.uniform(jax.random.fold_in(jax.random.fold_in(key, 6), dim), (blocks,), jnp.float32, low / len(shards), top_value / len(shards))
        level = level * jnp.repeat(jnp.exp(steps), extent[dim] // blocks).reshape((-1,) + (1,) * (len(extent) - 1 - dim))
    return level


def scatter_about(rng, extent, width, bound, pieces=(), kind=jnp.bfloat16):
    result = jax.random.normal(rng, extent, jnp.float32) * width
    if len(pieces) > 0:
        result = steps_of(rng, extent, pieces, -0.22, 0.18) * result
    return jnp.clip(result, min=-bound, max=bound).astype(kind)


def setup_inputs(seed: int = 0) -> dict:
    key_list = jax.random.split(jax.random.key(seed), 8)
    return {
        "out_grad": scatter_about(key_list[0], (N_SECTION, TOKENS, D), 1.0, 6.0, ((0, 8), (1, 32))),
        "router_weight": scatter_about(key_list[1], (N_SECTION, D, EXPERTS), (D // 16) ** -0.5, 0.25, ((0, 8),)),
        "down_weight": scatter_about(key_list[2], (N_SECTION, EXPERTS * HID, D), HID ** -0.5, 0.1875, ((0, 8), (1, 32))),
        "hidden_saved": scatter_about(key_list[3], (N_SECTION, N_EXPERT, N_EXPERT, CAP, HID_DEV), 0.25, 1.5, ((0, 8), (1, 32))),
        "slot_token": draw_slot_token(jax.random.fold_in(key_list[7], 71), 0),
        "slot_count": draw_slot_count(jax.random.fold_in(key_list[7], 71), 0),
        "slot_gate": jnp.clip(jnp.exp(math.log(1.0) - 3.912023 * jax.random.uniform(key_list[6], (N_SECTION, N_EXPERT, EXPERTS, CAP), jnp.float32) ** steps_of(key_list[6], (N_SECTION, N_EXPERT, EXPERTS, CAP), ((0, 8), (1, 32)), -0.2, 0.2)), 0.02, 1.0),
    }


def section_pass(grad, router, weight, saved, tokens, counts, gates):
    high = lax.Precision.HIGHEST
    grad_src = grad.reshape(N_EXPERT, TOK_DEV, D)
    slots = lax.broadcasted_iota(jnp.int32, (N_EXPERT, EXPERTS, CAP), 2)
    live = slots < counts[:, :, None]
    gate_live = jnp.where(live, gates, jnp.float32(0.0)).astype(jnp.float32)
    rows = jax.vmap(lambda g, t: g[t])(grad_src, tokens)
    rows = jnp.where(live[..., None], rows, jnp.zeros((), jnp.bfloat16))
    blocks = weight.reshape(N_EXPERT, HID_DEV, D)

    def per_owner(owner):
        expert_id = (owner // GROUP).astype(jnp.int32)
        block_rows = lax.dynamic_index_in_dim(rows, expert_id, 1, keepdims=False)
        block_gate = lax.dynamic_index_in_dim(gate_live, expert_id, 1, keepdims=False)
        w_block = lax.dynamic_index_in_dim(blocks, owner, 0, keepdims=False)
        held = lax.dynamic_index_in_dim(saved, owner, 0, keepdims=False)
        proj = jnp.einsum("scd,hd->sch", block_rows.astype(jnp.float32), w_block.astype(jnp.float32), precision=high)
        grad_hidden = (block_gate[..., None] * proj).astype(jnp.bfloat16)
        partial_value = jnp.sum(held.astype(jnp.float32) * proj, axis=-1)
        scaled = (block_gate[..., None] * block_rows.astype(jnp.float32)).astype(jnp.bfloat16)
        w_grad = jnp.einsum("sch,scd->hd", held.astype(jnp.float32), scaled.astype(jnp.float32), precision=high)
        return w_grad.astype(jnp.bfloat16), grad_hidden, partial_value

    w_grads, hidden_grads, partials = lax.map(per_owner, jnp.arange(N_EXPERT, dtype=jnp.int32))
    gate_grad = partials.reshape(EXPERTS, GROUP, N_EXPERT, CAP).sum(axis=1)
    gate_grad = jnp.transpose(gate_grad, (1, 0, 2))
    positions = lax.broadcasted_iota(jnp.int32, (N_EXPERT, EXPERTS, CAP, TOK_DEV), 3)
    match = jnp.where((tokens[..., None] == positions) & live[..., None], jnp.float32(1.0), jnp.float32(0.0))
    logit_grad = jnp.einsum("sec,sect->ste", gate_grad, match, precision=high).reshape(TOKENS, EXPERTS)
    input_grad = grad.astype(jnp.float32) + jnp.dot(logit_grad, router.astype(jnp.float32).T, precision=high)
    return w_grads.reshape(N_EXPERT * HID_DEV, D), hidden_grads, input_grad.astype(jnp.bfloat16)


def reference(out_grad, router_weight, down_weight, hidden_saved, slot_token, slot_count, slot_gate):
    down_grad, hidden_grad, input_grad = lax.map(
        lambda a: section_pass(*a),
        (out_grad, router_weight, down_weight, hidden_saved, slot_token, slot_count, slot_gate))
    zeros = jnp.zeros((1, TOKENS, D), jnp.bfloat16)
    passed_grad = jnp.concatenate([input_grad[1:], zeros], axis=0)
    return down_grad, hidden_grad, passed_grad
```

```python
import functools

import jax
import jax.numpy as jnp
from jax import lax
from jax.experimental import pallas as pl
from jax.experimental.pallas import tpu as pltpu
from jax.sharding import PartitionSpec as P

NX, NZ = 4, 8
TILE = 512
BF, F32 = jnp.bfloat16, jnp.float32


def shift_x(k):
    return [(x * NZ + z, (x + k) % NX * NZ + z) for x in range(NX) for z in range(NZ)]


def shift_z(k):
    return [(x * NZ + z, x * NZ + (z + k) % NZ) for x in range(NX) for z in range(NZ)]


def passed_along(value, axis, steps):
    count = lax.axis_size(axis)
    initial, last = (max(0, -steps), min(count, count - steps))
    return lax.ppermute(value, axis, [(source, source + steps) for source in range(initial, last)])


def rolled(value, start, axis):
    return lax.dynamic_slice_in_dim(jnp.concatenate([value, value], axis), start, value.shape[axis], axis)


def params():
    return pltpu.CompilerParams(vmem_limit_bytes=48 * 1024 * 1024)


def pick_rows(blocks, hots):
    n, cap, width = len(blocks), hots[0].shape[0] // NX, blocks[0].shape[1]
    tile = 1792

    def kernel(*refs):
        for b in range(n):
            got = jnp.dot(refs[n + b][...], refs[b][...], preferred_element_type=F32).astype(BF)
            for k in range(NX):
                refs[2 * n + k][b * cap : (b + 1) * cap, :] = got[k * cap : (k + 1) * cap]

    return pl.pallas_call(
        kernel,
        grid=(width // tile,),
        in_specs=[pl.BlockSpec((blocks[0].shape[0], tile), lambda j: (0, j))] * n
        + [pl.BlockSpec(hots[0].shape, lambda j: (0, 0))] * n,
        out_specs=[pl.BlockSpec((n * cap, tile), lambda j: (0, j))] * NX,
        out_shape=[jax.ShapeDtypeStruct((n * cap, width), BF)] * NX,
        compiler_params=params(),
        cost_estimate=pl.CostEstimate(
            flops=2 * n * NX * cap * 128 * width, bytes_accessed=4 * n * 128 * width, transcendentals=0
        ),
    )(*blocks, *hots)


def project(low, high, low_at, high_at, weight, held, gate):
    rows = low[0].shape[0]
    hid, width = weight.shape
    steps = width // 2 // TILE

    def kernel(*refs):
        lows, highs = refs[:NX], refs[NX : 2 * NX]
        w_low, w_high, held_ref, gate_ref, hid_ref, part_ref, acc = refs[2 * NX :]
        step = pl.program_id(0)
        contract = (((1,), (1,)), ((), ()))
        a = jnp.concatenate([r[...] for r in lows], 0)
        b = jnp.concatenate([r[...] for r in highs], 0)
        add = lax.dot_general(a, w_low[...], contract, preferred_element_type=F32)
        add += lax.dot_general(b, w_high[...], contract, preferred_element_type=F32)

        @pl.when(step == 0)
        def _():
            acc[...] = add

        @pl.when(step > 0)
        def _():
            acc[...] += add

        @pl.when(step == steps - 1)
        def _():
            proj = acc[...]
            hid_ref[...] = (gate_ref[...] * proj).astype(BF)
            part_ref[...] = jnp.sum((held_ref[...].astype(F32) * proj).T, axis=0, keepdims=True)

    def column(at):
        return pl.BlockSpec((rows, TILE), lambda j: (0, j + at // TILE))

    return pl.pallas_call(
        kernel,
        grid=(steps,),
        in_specs=[column(low_at)] * NX
        + [column(high_at)] * NX
        + [
            pl.BlockSpec((hid, TILE), lambda j: (0, j)),
            pl.BlockSpec((hid, TILE), lambda j: (0, j + steps)),
            pl.BlockSpec((NX * rows, hid), lambda j: (0, 0)),
            pl.BlockSpec((NX * rows, 1), lambda j: (0, 0)),
        ],
        out_specs=[
            pl.BlockSpec((NX * rows, hid), lambda j: (0, 0)),
            pl.BlockSpec((1, NX * rows), lambda j: (0, 0)),
        ],
        out_shape=[
            jax.ShapeDtypeStruct((NX * rows, hid), BF),
            jax.ShapeDtypeStruct((1, NX * rows), F32),
        ],
        scratch_shapes=[pltpu.VMEM((NX * rows, hid), F32)],
        compiler_params=params(),
        cost_estimate=pl.CostEstimate(
            flops=2 * NX * rows * hid * width,
            bytes_accessed=2 * width * (hid + NX * rows),
            transcendentals=0,
        ),
    )(*low, *high, weight, weight, held, gate)


def weight_grad(rows, at, held_t, half, width, before):
    hid, total = held_t.shape
    steps = width // 2 // TILE
    n = len(rows)

    def kernel(*refs):
        a = jnp.concatenate([r[...] for r in refs[:n]], 0)
        refs[-1][...] = jnp.dot(refs[n][...], a, preferred_element_type=F32).astype(BF)

    def column(r, start):
        return pl.BlockSpec((r.shape[0], TILE), lambda j: (0, j + start // TILE))

    extra = [] if before is None else [before]
    return pl.pallas_call(
        kernel,
        grid=(steps,),
        in_specs=[column(r, s) for r, s in zip(rows, at)]
        + [pl.BlockSpec((hid, total), lambda j: (0, 0))]
        + [pl.BlockSpec(memory_space=pl.ANY) for _ in extra],
        out_specs=pl.BlockSpec((hid, TILE), lambda j: (0, j + half * steps)),
        out_shape=jax.ShapeDtypeStruct((hid, width), BF),
        input_output_aliases={n + 1: 0} if extra else {},
        compiler_params=params(),
        cost_estimate=pl.CostEstimate(
            flops=total * hid * width, bytes_accessed=width * (hid + total), transcendentals=0
        ),
    )(*rows, held_t, *extra)


def shards(out_grad, router_weight, down_weight, hidden_saved, slot_token, slot_count, slot_gate):
    high = lax.Precision.HIGHEST
    grad = out_grad[0]
    tokens = slot_token[0, 0]
    counts = slot_count[0, 0]
    gates = slot_gate[0, 0]
    w_block = down_weight[0]
    experts, capacity = tokens.shape
    tok_count, width = grad.shape
    hid = w_block.shape[0]
    group = lax.axis_size("expert") // experts
    mid = width // 2
    me = lax.axis_index("expert")
    mx, mz = me // NZ, me % NZ

    slots = lax.broadcasted_iota(jnp.int32, (experts, capacity), 1)
    live = slots < counts[:, None]
    gate_live = jnp.where(live, gates, F32(0.0))
    token_live = jnp.where(live, tokens, -1).astype(F32)

    with jax.named_scope("next_section"):
        grad_next = passed_along(grad, "section", -1)
        router_next = passed_along(router_weight[0].T, "section", -1)

    with jax.named_scope("slots"):
        by_half = token_live.reshape(NX, 2, capacity).transpose(1, 0, 2)
        line = [[x * NZ + z for z in range(NZ)] for x in range(NX)]
        spread = jnp.broadcast_to(by_half[:, None], (2, NZ // 2, NX, capacity)).reshape(NZ, NX, capacity)
        got_tokens = lax.all_to_all(
            spread, "expert", split_axis=0, concat_axis=0, axis_index_groups=line, tiled=True
        )
        own_tokens = rolled(lax.dynamic_index_in_dim(by_half, mz // (NZ // 2), 0, False), mx, 0)
        got_tokens = rolled(rolled(got_tokens, mz, 0), mx, 1)
        gate_sent = jnp.broadcast_to(gate_live[:, None], (experts, group, capacity)).reshape(
            experts * group, capacity
        )
        got_gate = lax.all_to_all(gate_sent, "expert", split_axis=0, concat_axis=0, tiled=True)

    def one_hot(ids):
        ids = ids.reshape(-1, NX * capacity)
        places = lax.broadcasted_iota(jnp.int32, ids.shape + (tok_count,), 2).astype(F32)
        return jnp.where(ids[..., None] == places, F32(1.0), F32(0.0)).astype(BF)

    hot_own = one_hot(own_tokens)[0]
    hots = one_hot(got_tokens)

    def exchanged(picked):
        return [picked[0]] + [lax.ppermute(picked[k], "expert", shift_x(k)) for k in range(1, NX)]

    last = NZ // 2
    order = [(0, [0])] + [(t, [NZ - t, t]) for t in range(1, last)] + [(last, [last])]
    halves = (grad[:, :mid], grad[:, mid:])
    with jax.named_scope("own_rows"):
        arrived = {(0, h): exchanged(pick_rows([grad], [hot_own])) for h in (0,)}
    arrived[0, 1] = arrived[0, 0]
    up, down = dict(enumerate(halves)), dict(enumerate(halves))
    for t in range(1, last + 1):
        for h in (0, 1):
            with jax.named_scope("ring_z"):
                if t < last or h == 0:
                    up[h] = lax.ppermute(up[h], "expert", shift_z(1))
                if t < last or h == 1:
                    down[h] = lax.ppermute(down[h], "expert", shift_z(-1))
            with jax.named_scope("exchange_x"):
                if t < last:
                    picked = pick_rows([up[h], down[h]], [hots[NZ - t], hots[t]])
                else:
                    picked = pick_rows([up[h] if h == 0 else down[h]], [hots[last]])
                arrived[t, h] = exchanged(picked)

    with jax.named_scope("held"):
        held = rolled(rolled(hidden_saved[0, 0].reshape(NX, NZ, capacity, hid), mx, 0), mz, 1)
        gate_r = rolled(rolled(got_gate.reshape(NX, NZ, capacity), mx, 0), mz, 1)
        pieces = [(t, (NX - k) % NX, d) for t, ds in order for k in range(NX) for d in ds]
        held_p = jnp.concatenate([held[k, d] for _, k, d in pieces], 0)
        gate_p = jnp.concatenate([gate_r[k, d] for _, k, d in pieces], 0)[:, None]
        held_t = (held_p.astype(F32) * gate_p).astype(BF).T

    hidden, partial = {}, {}
    at = 0
    for t, ds in order:
        n = NX * len(ds) * capacity
        with jax.named_scope("project"):
            hg, part = project(
                arrived[t, 0],
                arrived[t, 1],
                0,
                mid if t == 0 else 0,
                w_block,
                held_p[at : at + n],
                gate_p[at : at + n],
            )
        hg = hg.reshape(NX, len(ds), capacity, hid)
        part = part.reshape(NX, len(ds), capacity)
        for k in range(NX):
            for i, d in enumerate(ds):
                hidden[(NX - k) % NX, d] = hg[k, i]
                partial[(NX - k) % NX, d] = part[k, i]
        at += n

    def by_source(table):
        full = jnp.stack([jnp.stack([table[k, d] for d in range(NZ)], 0) for k in range(NX)], 0)
        full = rolled(rolled(full, (NX - mx) % NX, 0), (NZ - mz) % NZ, 1)
        return full.reshape((NX * NZ,) + full.shape[2:])

    with jax.named_scope("gate_return"):
        returned = lax.all_to_all(by_source(partial), "expert", split_axis=0, concat_axis=0, tiled=True)
    hidden_grad = by_source(hidden)

    with jax.named_scope("weight_grad"):
        down_grad = None
        for h in (0, 1):
            rows = [r for t, _ in order for r in arrived[t, h]]
            starts = [mid if t == 0 and h == 1 else 0 for t, _ in order for _ in range(NX)]
            down_grad = weight_grad(rows, starts, held_t, h, width, down_grad)

    with jax.named_scope("input_grad"):
        gate_grad = returned.reshape(experts, group, capacity).sum(axis=1)
        positions = lax.broadcasted_iota(jnp.int32, (experts, capacity, tok_count), 2)
        match = jnp.where(
            (tokens[..., None] == positions) & live[..., None], F32(1.0), F32(0.0)
        )
        logit_grad = jnp.einsum("ec,ect->te", gate_grad, match, precision=high)
        logit_next = passed_along(logit_grad, "section", -1)
        passed = grad_next.astype(F32) + jnp.dot(logit_next, router_next.astype(F32), precision=high)
    return (down_grad[None], hidden_grad[None, None], passed.astype(BF)[None])


def solution(mesh):
    return jax.shard_map(
        shards,
        mesh=mesh,
        in_specs=(
            P("section", "expert", None),
            P("section", None, None),
            P("section", "expert", None),
            P("section", "expert", None, None, None),
            P("section", "expert", None, None),
            P("section", "expert", None),
            P("section", "expert", None, None),
        ),
        out_specs=(
            P("section", "expert", None),
            P("section", "expert", None, None, None),
            P("section", "expert", None),
        ),
        check_vma=False,
    )
```

```python
import jax
import jax.numpy as jnp
from jax import lax
from jax.experimental import pallas as pl
from jax.experimental.pallas import tpu as pltpu
from jax.sharding import PartitionSpec as P

NX, NZ = 4, 8
TILE = 1792
WIDE = 1792
LANES = 128
META = 4
BF, F32 = jnp.bfloat16, jnp.float32


def shift_x(k):
    return [(x * NZ + z, (x + k) % NX * NZ + z) for x in range(NX) for z in range(NZ)]


def shift_z(k):
    return [(x * NZ + z, x * NZ + (z + k) % NZ) for x in range(NX) for z in range(NZ)]


def passed_along(value, axis, steps):
    count = lax.axis_size(axis)
    initial, last = (max(0, -steps), min(count, count - steps))
    return lax.ppermute(value, axis, [(source, source + steps) for source in range(initial, last)])


def call(kernel, grid, in_specs, out_specs, out_shape, scratch=(), aliases=None, flops=0, nbytes=0, vmem=63):
    return pl.pallas_call(
        kernel,
        grid_spec=pltpu.PrefetchScalarGridSpec(
            num_scalar_prefetch=1,
            grid=grid,
            in_specs=in_specs,
            out_specs=out_specs,
            scratch_shapes=list(scratch),
        ),
        out_shape=out_shape,
        input_output_aliases=aliases or {},
        compiler_params=pltpu.CompilerParams(vmem_limit_bytes=vmem * 1024 * 1024),
        cost_estimate=pl.CostEstimate(flops=flops, bytes_accessed=nbytes, transcendentals=0),
    )


def whole(shape):
    return pl.BlockSpec(shape, lambda j, w: (0,) * len(shape))


def columns(rows, tile, start):
    return pl.BlockSpec((rows, tile), lambda j, w: (0, j + start // tile))


HBM = pl.BlockSpec(memory_space=pl.ANY)


def picked(w_ref, meta, parts, outs, at_row):
    slots, tokens = meta.shape[0], parts[0].shape[0]
    cap = slots // NX
    half = w_ref[1] // (NZ // 2)
    lane = lax.broadcasted_iota(jnp.int32, (slots, LANES), 1)
    wanted = jnp.sum(jnp.where(lane == META * half, meta.astype(F32), F32(0.0)), axis=1, keepdims=True)
    place = lax.broadcasted_iota(jnp.int32, (slots, tokens), 1).astype(F32)
    hot = jnp.where(wanted == place, F32(1.0), F32(0.0)).astype(BF)
    at = 0
    for part in parts:
        got = jnp.dot(hot, part[...], preferred_element_type=F32).astype(BF)
        for k in range(NX):
            outs[k][at_row : at_row + cap, at : at + part.shape[1]] = got[k * cap : (k + 1) * cap]
        at += part.shape[1]
    for k in range(NX):
        outs[k][at_row : at_row + cap, at:] = meta[k * cap : (k + 1) * cap]


def begin(where, grad, tokens, gates):
    count, width = grad.shape
    cap = tokens.shape[1]

    def kernel(w_ref, g_ref, t_ref, s_ref, block_ref, *outs):
        block_ref[:, :width] = g_ref[...]
        block_ref[:, width:] = jnp.zeros((count, LANES), BF)
        slot = lax.broadcasted_iota(jnp.int32, (1, cap), 1)
        for k in range(NX):
            lines = []
            for half in (0, 1):
                e = lax.rem(w_ref[0] + k, NX) * 2 + half
                live = slot < w_ref[2 + e]
                lines.append(jnp.where(live, t_ref[pl.ds(e, 1), :], -1).astype(F32))
                rest = jnp.where(live, s_ref[pl.ds(e, 1), :], F32(0.0))
                for _ in range(META - 1):
                    piece = rest.astype(BF).astype(F32)
                    lines.append(piece)
                    rest = rest - piece
            table = jnp.concatenate(lines, 0)
            table = jnp.concatenate([table, jnp.zeros((2 * META, LANES - cap), F32)], 1)
            table = jnp.concatenate([table, jnp.zeros((LANES - 2 * META, LANES), F32)], 0).T
            block_ref[k * cap : (k + 1) * cap, width:] = table[:cap].astype(BF)
        picked(w_ref, block_ref[:, width:], [g_ref], outs, 0)

    full = width + LANES
    return call(
        kernel,
        (1,),
        [whole(x.shape) for x in (grad, tokens, gates)],
        [whole((count, full))] + [whole((cap, full))] * NX,
        [jax.ShapeDtypeStruct((count, full), BF)] + [jax.ShapeDtypeStruct((cap, full), BF)] * NX,
        flops=2 * NX * cap * count * width,
        nbytes=6 * count * width,
    )(where, grad, tokens, gates)


def pick_rows(where, blocks, after):
    n = len(blocks)
    flat = [x for block in blocks for x in block]
    tokens = flat[0].shape[0]
    full = sum(x.shape[1] for x in blocks[0])
    cap = tokens // NX

    def kernel(w_ref, *refs):
        outs = refs[-NX:]
        for b in range(n):
            parts = list(refs[b * len(blocks[b]) : (b + 1) * len(blocks[b])])
            cut = parts[-1].shape[1] - LANES
            meta = parts[-1][:, cut:]
            parts[-1] = parts[-1].at[:, :cut]
            picked(w_ref, meta, parts, outs, b * cap)

    return call(
        kernel,
        (1,),
        [whole(x.shape) for x in flat] + [HBM] * len(after),
        [whole((n * cap, full))] * NX,
        [jax.ShapeDtypeStruct((n * cap, full), BF)] * NX,
        flops=2 * n * tokens * tokens * full,
        nbytes=4 * n * tokens * full,
    )(where, *flat, *after)


def hold(arrays, after):
    n = len(arrays)
    return pl.pallas_call(
        lambda *refs: None,
        in_specs=[HBM] * (n + len(after)),
        out_specs=[HBM] * n,
        out_shape=[jax.ShapeDtypeStruct(x.shape, x.dtype) for x in arrays],
        input_output_aliases={i: i for i in range(n)},
    )(*arrays, *after)


def project(where, got, weight, held, shifts, before):
    rows = got[0].shape[0]
    hid, width = weight.shape
    cap = rows // len(shifts)
    steps = width // 2 // TILE
    n = NX * len(shifts)

    def kernel(w_ref, *refs):
        lows, highs, metas = refs[:NX], refs[NX : 2 * NX], refs[2 * NX : 3 * NX]
        w_low, w_high, held_hbm = refs[3 * NX : 3 * NX + 3]
        hid_hbm, part_hbm, scaled_ref, acc, held_v, hid_v, part_v, sem_in, sem_hid, sem_part = refs[-10:]
        step = pl.program_id(0)

        def source(j):
            k, d = j // len(shifts), shifts[j % len(shifts)]
            return lax.rem(w_ref[0] + (NX - k), NX) * NZ + lax.rem(w_ref[1] + d, NZ)

        fetch = [pltpu.make_async_copy(held_hbm.at[source(j)], held_v.at[j], sem_in.at[j]) for j in range(n)]

        @pl.when(step == 0)
        def _():
            for copy in fetch:
                copy.start()

        contract = (((1,), (1,)), ((), ()))
        a = jnp.concatenate([r[...] for r in lows], 0)
        b = jnp.concatenate([r[...] for r in highs], 0)
        add = lax.dot_general(a, w_low[...], contract, preferred_element_type=F32)
        add += lax.dot_general(b, w_high[...], contract, preferred_element_type=F32)

        @pl.when(step == 0)
        def _():
            acc[...] = add

        @pl.when(step > 0)
        def _():
            acc[...] += add

        @pl.when(step == steps - 1)
        def _():
            half = w_ref[1] // (NZ // 2)
            lane = lax.broadcasted_iota(jnp.int32, (rows, LANES), 1) - META * half
            is_gate = (lane >= 1) & (lane < META)
            gate = jnp.concatenate(
                [
                    jnp.sum(jnp.where(is_gate, m[...].astype(F32), F32(0.0)), axis=1, keepdims=True)
                    for m in metas
                ],
                0,
            )
            proj = acc[...]
            hid_v[...] = (gate * proj).astype(BF).reshape(n, cap, hid)
            for copy in fetch:
                copy.wait()
            held_f = held_v[...].reshape(n * cap, hid).astype(F32)
            scaled_ref[...] = (held_f * gate).T.astype(BF)
            both = held_f * proj
            for j in range(n):
                part_v[j] = jnp.sum(both[j * cap : (j + 1) * cap].T, axis=0, keepdims=True)
            stores = []
            for j in range(n):
                stores.append(pltpu.make_async_copy(hid_v.at[j], hid_hbm.at[source(j)], sem_hid.at[j]))
                stores.append(pltpu.make_async_copy(part_v.at[j], part_hbm.at[source(j)], sem_part.at[j]))
            for copy in stores:
                copy.start()
            for copy in stores:
                copy.wait()

    extra = list(before) if before else []
    first = 1 + 3 * NX + 3
    sources = held.shape[0]
    return call(
        kernel,
        (steps,),
        [columns(rows, TILE, 0)] * NX
        + [columns(rows, TILE, width // 2)] * NX
        + [pl.BlockSpec((rows, LANES), lambda j, w: (0, width // LANES))] * NX
        + [columns(hid, TILE, 0), columns(hid, TILE, width // 2), HBM]
        + [HBM] * len(extra),
        [HBM, HBM, whole((hid, n * cap))],
        [
            jax.ShapeDtypeStruct(held.shape, BF),
            jax.ShapeDtypeStruct((sources, 1, cap), F32),
            jax.ShapeDtypeStruct((hid, n * cap), BF),
        ],
        [
            pltpu.VMEM((n * cap, hid), F32),
            pltpu.VMEM((n, cap, hid), BF),
            pltpu.VMEM((n, cap, hid), BF),
            pltpu.VMEM((n, 1, cap), F32),
            pltpu.SemaphoreType.DMA((n,)),
            pltpu.SemaphoreType.DMA((n,)),
            pltpu.SemaphoreType.DMA((n,)),
        ],
        {first: 0, first + 1: 1} if extra else {},
        flops=2 * n * cap * hid * width,
        nbytes=2 * width * (hid + n * cap),
    )(where, *got, *got, *got, weight, weight, held, *extra)


def weight_grad(where, rows, scaled, width):
    hid = scaled[0].shape[0]
    n, m = len(rows), len(scaled)
    total = sum(r.shape[0] for r in rows)

    def kernel(w_ref, *refs):
        b = jnp.concatenate([r[...] for r in refs[:n]], 0)
        a = jnp.concatenate([r[...] for r in refs[n : n + m]], 1)
        refs[-1][...] = jnp.dot(a, b, preferred_element_type=F32).astype(BF)

    return call(
        kernel,
        (width // WIDE,),
        [columns(r.shape[0], WIDE, 0) for r in rows] + [whole(x.shape) for x in scaled],
        columns(hid, WIDE, 0),
        jax.ShapeDtypeStruct((hid, width), BF),
        flops=2 * total * hid * width,
        nbytes=2 * width * (hid + total),
    )(where, *rows, *scaled)


def finish(where, grad, router, logit):
    rows, width = grad.shape

    def kernel(w_ref, g_ref, r_ref, l_ref, out_ref):
        piece = l_ref[...].astype(F32).T.astype(BF)
        add = jnp.dot(piece, r_ref[...], preferred_element_type=F32)
        out_ref[...] = (g_ref[...].astype(F32) + add).astype(BF)

    return call(
        kernel,
        (2,),
        [columns(rows, width // 2, 0), columns(router.shape[0], width // 2, 0), whole(logit.shape)],
        columns(rows, width // 2, 0),
        jax.ShapeDtypeStruct((rows, width), BF),
        flops=2 * rows * width * router.shape[0],
        nbytes=4 * rows * width,
        vmem=16,
    )(where, grad, router, logit)


def logits(returned, match, after):
    owners, _, cap = returned.shape
    experts = match.shape[0] // cap
    group = owners // experts

    def kernel(r_ref, m_ref, *refs):
        lines = []
        for e in range(experts):
            lines.append(sum(r_ref[e * group + q] for q in range(group)))
        gate = jnp.concatenate([jnp.concatenate(lines, 0)] * experts, 1)
        row = lax.broadcasted_iota(jnp.int32, gate.shape, 0)
        lane = lax.broadcasted_iota(jnp.int32, gate.shape, 1)
        rest = jnp.where(lane // cap == row, gate, F32(0.0))
        for i in range(3):
            piece = rest.astype(BF)
            rest = rest - piece.astype(F32)
            got = jnp.dot(piece, m_ref[...], preferred_element_type=F32)
            refs[-1][i * experts : (i + 1) * experts, :] = got.astype(BF)

    return pl.pallas_call(
        kernel,
        in_specs=[pl.BlockSpec(memory_space=pltpu.VMEM)] * 2 + [HBM] * len(after),
        out_specs=pl.BlockSpec(memory_space=pltpu.VMEM),
        out_shape=jax.ShapeDtypeStruct((3 * experts, match.shape[1]), BF),
    )(returned, match, *after)


def shards(out_grad, router_weight, down_weight, hidden_saved, slot_token, slot_count, slot_gate):
    grad = out_grad[0]
    tokens = slot_token[0, 0]
    counts = slot_count[0, 0]
    gates = slot_gate[0, 0]
    weight = down_weight[0]
    held = hidden_saved[0, 0]
    experts, capacity = tokens.shape
    tok_count, width = grad.shape
    mid = width // 2
    me = lax.axis_index("expert")
    mx, mz = me // NZ, me % NZ
    where = jnp.stack([mx, mz]).astype(jnp.int32)

    where = jnp.concatenate([jnp.stack([mx, mz]).astype(jnp.int32), counts])

    with jax.named_scope("next_section"):
        grad_next = passed_along(grad, "section", -1)
        router_next = passed_along(router_weight[0].T, "section", -1)
        router_next = jnp.concatenate([router_next] * 3, 0)

    def exchanged(rows):
        with jax.named_scope("exchange_x"):
            return [rows[0]] + [lax.ppermute(rows[k], "expert", shift_x(k)) for k in range(1, NX)]

    last = NZ // 2
    order = [[0]] + [[NZ - t, t] for t in range(1, last)] + [[last]]
    with jax.named_scope("pick"):
        block, *rows = begin(where, grad, tokens, gates)
    up = down = block
    arrived, scaled, written = [exchanged(rows)], [], None
    for t in range(1, last + 1):
        with jax.named_scope("ring_z"):
            if t == last:
                up, down = up[:, :mid], down[:, mid:]
            up = lax.ppermute(up, "expert", shift_z(1))
            down = lax.ppermute(down, "expert", shift_z(-1))
        with jax.named_scope("pick"):
            rows = pick_rows(where, [[up], [down]] if t < last else [[up, down]], scaled[t - 2 : t - 1])
            if t < last:
                up, down = hold([up, down], arrived[t - 1][1:] + [rows[0]])
            arrived.append(exchanged(rows))
        with jax.named_scope("project"):
            *written, piece = project(where, arrived[t - 1], weight, held, order[t - 1], written)
        scaled.append(piece)
    with jax.named_scope("project"):
        *written, piece = project(where, arrived[last], weight, held, order[last], written)
    scaled.append(piece)
    hidden_grad, partial = written

    with jax.named_scope("gate_return"):
        returned = lax.all_to_all(partial, "expert", split_axis=0, concat_axis=0, tiled=True)

    with jax.named_scope("weight_grad"):
        down_grad = weight_grad(where, [r for rows in arrived for r in rows], scaled, width)

    with jax.named_scope("input_grad"):
        slots = lax.broadcasted_iota(jnp.int32, (experts, capacity), 1)
        spot = jnp.where(slots < counts[:, None], tokens, -1).reshape(-1, 1)
        match = (spot == lax.broadcasted_iota(jnp.int32, (1, tok_count), 1)).astype(BF)
        logit_grad = logits(returned, match, [down_grad])
        logit_next = passed_along(logit_grad, "section", -1)
        passed = finish(where, grad_next, router_next, logit_next)
    return (down_grad[None], hidden_grad[None, None], passed[None])


def solution(mesh):
    return jax.shard_map(
        shards,
        mesh=mesh,
        in_specs=(
            P("section", "expert", None),
            P("section", None, None),
            P("section", "expert", None),
            P("section", "expert", None, None, None),
            P("section", "expert", None, None),
            P("section", "expert", None),
            P("section", "expert", None, None),
        ),
        out_specs=(
            P("section", "expert", None),
            P("section", "expert", None, None, None),
            P("section", "expert", None),
        ),
        check_vma=False,
    )
```

```python
import jax
import jax.numpy as jnp
from jax import lax
from jax.experimental import pallas as pl
from jax.experimental.pallas import tpu as pltpu
from jax.sharding import PartitionSpec as P

NX, NZ = 4, 8
TILE = 1792
WIDE = 1792
LANES = 128
META = 4
BF, F32 = jnp.bfloat16, jnp.float32


def shift_x(k):
    return [(x * NZ + z, (x + k) % NX * NZ + z) for x in range(NX) for z in range(NZ)]


def shift_z(k):
    return [(x * NZ + z, x * NZ + (z + k) % NZ) for x in range(NX) for z in range(NZ)]


def passed_along(value, axis, steps):
    count = lax.axis_size(axis)
    initial, last = (max(0, -steps), min(count, count - steps))
    return lax.ppermute(value, axis, [(source, source + steps) for source in range(initial, last)])


def call(kernel, grid, in_specs, out_specs, out_shape, scratch=(), aliases=None, flops=0, nbytes=0, vmem=63):
    return pl.pallas_call(
        kernel,
        grid_spec=pltpu.PrefetchScalarGridSpec(
            num_scalar_prefetch=1,
            grid=grid,
            in_specs=in_specs,
            out_specs=out_specs,
            scratch_shapes=list(scratch),
        ),
        out_shape=out_shape,
        input_output_aliases=aliases or {},
        compiler_params=pltpu.CompilerParams(vmem_limit_bytes=vmem * 1024 * 1024),
        cost_estimate=pl.CostEstimate(flops=flops, bytes_accessed=nbytes, transcendentals=0),
    )


def whole(shape):
    return pl.BlockSpec(shape, lambda j, w: (0,) * len(shape))


def columns(rows, tile, start):
    return pl.BlockSpec((rows, tile), lambda j, w: (0, j + start // tile))


HBM = pl.BlockSpec(memory_space=pl.ANY)


def picked(w_ref, meta, parts, outs, at_row):
    slots, tokens = meta.shape[0], parts[0].shape[0]
    cap = slots // NX
    half = w_ref[1] // (NZ // 2)
    lane = lax.broadcasted_iota(jnp.int32, (slots, LANES), 1)
    wanted = jnp.sum(jnp.where(lane == META * half, meta.astype(F32), F32(0.0)), axis=1, keepdims=True)
    place = lax.broadcasted_iota(jnp.int32, (slots, tokens), 1).astype(F32)
    hot = jnp.where(wanted == place, F32(1.0), F32(0.0)).astype(BF)
    at = 0
    for part in parts:
        got = jnp.dot(hot, part[...], preferred_element_type=F32).astype(BF)
        for k in range(NX):
            outs[k][at_row : at_row + cap, at : at + part.shape[1]] = got[k * cap : (k + 1) * cap]
        at += part.shape[1]
    for k in range(NX):
        outs[k][at_row : at_row + cap, at:] = meta[k * cap : (k + 1) * cap]


def begin(where, grad, tokens, gates):
    count, width = grad.shape
    cap = tokens.shape[1]

    def kernel(w_ref, g_ref, t_ref, s_ref, meta_ref, *outs):
        slot = lax.broadcasted_iota(jnp.int32, (1, cap), 1)
        for k in range(NX):
            lines = []
            for half in (0, 1):
                e = lax.rem(w_ref[0] + k, NX) * 2 + half
                live = slot < w_ref[2 + e]
                lines.append(jnp.where(live, t_ref[pl.ds(e, 1), :], -1).astype(F32))
                rest = jnp.where(live, s_ref[pl.ds(e, 1), :], F32(0.0))
                for _ in range(META - 1):
                    piece = rest.astype(BF).astype(F32)
                    lines.append(piece)
                    rest = rest - piece
            table = jnp.concatenate(lines, 0)
            table = jnp.concatenate([table, jnp.zeros((2 * META, LANES - cap), F32)], 1)
            table = jnp.concatenate([table, jnp.zeros((LANES - 2 * META, LANES), F32)], 0).T
            for z in range(NZ):
                meta_ref[z, k * cap : (k + 1) * cap, :] = table[:cap].astype(BF)
        picked(w_ref, meta_ref[0], [g_ref], outs, 0)

    full = width + LANES
    return call(
        kernel,
        (1,),
        [whole(x.shape) for x in (grad, tokens, gates)],
        [whole((NZ, NX * cap, LANES))] + [whole((cap, full))] * NX,
        [jax.ShapeDtypeStruct((NZ, NX * cap, LANES), BF)] + [jax.ShapeDtypeStruct((cap, full), BF)] * NX,
        flops=2 * NX * cap * count * width,
        nbytes=6 * count * width,
    )(where, grad, tokens, gates)


def pick_rows(where, blocks, metas, places, after, cut):
    n = len(blocks)
    flat = [x for block in blocks for x in block]
    tokens = flat[0].shape[0]
    width = sum(x.shape[1] for x in blocks[0])
    slots = metas.shape[1]
    cap = slots // NX
    mid = width // 2
    cuts = 2 if cut else 0

    def kernel(w_ref, *refs):
        outs = refs[len(refs) - NX - cuts :]
        for b in range(n):
            parts = refs[b * len(blocks[b]) : (b + 1) * len(blocks[b])]
            picked(w_ref, refs[len(flat) + b][0], parts, outs[:NX], b * cap)
        if cut:
            outs[NX][...] = refs[0][:, :mid]
            outs[NX + 1][...] = refs[1][:, mid:]

    shapes = [(n * cap, width + LANES)] * NX + [(tokens, mid)] * cuts
    return call(
        kernel,
        (1,),
        [whole(x.shape) for x in flat]
        + [pl.BlockSpec((1, slots, LANES), lambda j, w, d=d: (lax.rem(w[1] + d, NZ), 0, 0)) for d in places]
        + [HBM] * len(after),
        [whole(x) for x in shapes],
        [jax.ShapeDtypeStruct(x, BF) for x in shapes],
        flops=2 * n * slots * tokens * width,
        nbytes=4 * n * tokens * width,
    )(where, *flat, *[metas] * n, *after)


def hold(arrays, after):
    n = len(arrays)
    return pl.pallas_call(
        lambda *refs: None,
        in_specs=[HBM] * (n + len(after)),
        out_specs=[HBM] * n,
        out_shape=[jax.ShapeDtypeStruct(x.shape, x.dtype) for x in arrays],
        input_output_aliases={i: i for i in range(n)},
    )(*arrays, *after)


def project(where, got, weight, held, shifts, before):
    rows = got[0].shape[0]
    hid, width = weight.shape
    cap = rows // len(shifts)
    steps = width // 2 // TILE
    n = NX * len(shifts)

    def kernel(w_ref, *refs):
        lows, highs, metas = refs[:NX], refs[NX : 2 * NX], refs[2 * NX : 3 * NX]
        w_low, w_high, held_hbm = refs[3 * NX : 3 * NX + 3]
        hid_hbm, part_hbm, scaled_ref, acc, held_v, hid_v, part_v, sem_in, sem_hid, sem_part = refs[-10:]
        step = pl.program_id(0)

        def source(j):
            k, d = j // len(shifts), shifts[j % len(shifts)]
            return lax.rem(w_ref[0] + (NX - k), NX) * NZ + lax.rem(w_ref[1] + d, NZ)

        fetch = [pltpu.make_async_copy(held_hbm.at[source(j)], held_v.at[j], sem_in.at[j]) for j in range(n)]

        @pl.when(step == 0)
        def _():
            for copy in fetch:
                copy.start()

        contract = (((1,), (1,)), ((), ()))
        a = jnp.concatenate([r[...] for r in lows], 0)
        b = jnp.concatenate([r[...] for r in highs], 0)
        add = lax.dot_general(a, w_low[...], contract, preferred_element_type=F32)
        add += lax.dot_general(b, w_high[...], contract, preferred_element_type=F32)

        @pl.when(step == 0)
        def _():
            acc[...] = add

        @pl.when(step > 0)
        def _():
            acc[...] += add

        @pl.when(step == steps - 1)
        def _():
            half = w_ref[1] // (NZ // 2)
            lane = lax.broadcasted_iota(jnp.int32, (rows, LANES), 1) - META * half
            is_gate = (lane >= 1) & (lane < META)
            gate = jnp.concatenate(
                [
                    jnp.sum(jnp.where(is_gate, m[...].astype(F32), F32(0.0)), axis=1, keepdims=True)
                    for m in metas
                ],
                0,
            )
            proj = acc[...]
            hid_v[...] = (gate * proj).astype(BF).reshape(n, cap, hid)
            for copy in fetch:
                copy.wait()
            held_f = held_v[...].reshape(n * cap, hid).astype(F32)
            scaled_ref[...] = (held_f * gate).T.astype(BF)
            both = held_f * proj
            for j in range(n):
                part_v[j] = jnp.sum(both[j * cap : (j + 1) * cap].T, axis=0, keepdims=True)
            stores = []
            for j in range(n):
                stores.append(pltpu.make_async_copy(hid_v.at[j], hid_hbm.at[source(j)], sem_hid.at[j]))
                stores.append(pltpu.make_async_copy(part_v.at[j], part_hbm.at[source(j)], sem_part.at[j]))
            for copy in stores:
                copy.start()
            for copy in stores:
                copy.wait()

    extra = list(before) if before else []
    first = 1 + 3 * NX + 3
    sources = held.shape[0]
    return call(
        kernel,
        (steps,),
        [columns(rows, TILE, 0)] * NX
        + [columns(rows, TILE, width // 2)] * NX
        + [pl.BlockSpec((rows, LANES), lambda j, w: (0, width // LANES))] * NX
        + [columns(hid, TILE, 0), columns(hid, TILE, width // 2), HBM]
        + [HBM] * len(extra),
        [HBM, HBM, whole((hid, n * cap))],
        [
            jax.ShapeDtypeStruct(held.shape, BF),
            jax.ShapeDtypeStruct((sources, 1, cap), F32),
            jax.ShapeDtypeStruct((hid, n * cap), BF),
        ],
        [
            pltpu.VMEM((n * cap, hid), F32),
            pltpu.VMEM((n, cap, hid), BF),
            pltpu.VMEM((n, cap, hid), BF),
            pltpu.VMEM((n, 1, cap), F32),
            pltpu.SemaphoreType.DMA((n,)),
            pltpu.SemaphoreType.DMA((n,)),
            pltpu.SemaphoreType.DMA((n,)),
        ],
        {first: 0, first + 1: 1} if extra else {},
        flops=2 * n * cap * hid * width,
        nbytes=2 * width * (hid + n * cap),
    )(where, *got, *got, *got, weight, weight, held, *extra)


def weight_grad(where, rows, scaled, width):
    hid = scaled[0].shape[0]
    n, m = len(rows), len(scaled)
    total = sum(r.shape[0] for r in rows)

    def kernel(w_ref, *refs):
        b = jnp.concatenate([r[...] for r in refs[:n]], 0)
        a = jnp.concatenate([r[...] for r in refs[n : n + m]], 1)
        refs[-1][...] = jnp.dot(a, b, preferred_element_type=F32).astype(BF)

    return call(
        kernel,
        (width // WIDE,),
        [columns(r.shape[0], WIDE, 0) for r in rows] + [whole(x.shape) for x in scaled],
        columns(hid, WIDE, 0),
        jax.ShapeDtypeStruct((hid, width), BF),
        flops=2 * total * hid * width,
        nbytes=2 * width * (hid + total),
    )(where, *rows, *scaled)


def finish(where, grad, router, logit):
    rows, width = grad.shape

    def kernel(w_ref, g_ref, r_ref, l_ref, out_ref):
        piece = l_ref[...].astype(F32).T.astype(BF)
        add = jnp.dot(piece, r_ref[...], preferred_element_type=F32)
        out_ref[...] = (g_ref[...].astype(F32) + add).astype(BF)

    return call(
        kernel,
        (2,),
        [columns(rows, width // 2, 0), columns(router.shape[0], width // 2, 0), whole(logit.shape)],
        columns(rows, width // 2, 0),
        jax.ShapeDtypeStruct((rows, width), BF),
        flops=2 * rows * width * router.shape[0],
        nbytes=4 * rows * width,
        vmem=16,
    )(where, grad, router, logit)


def logits(returned, match, after):
    owners, _, cap = returned.shape
    experts = match.shape[0] // cap
    group = owners // experts

    def kernel(r_ref, m_ref, *refs):
        lines = []
        for e in range(experts):
            lines.append(sum(r_ref[e * group + q] for q in range(group)))
        gate = jnp.concatenate([jnp.concatenate(lines, 0)] * experts, 1)
        row = lax.broadcasted_iota(jnp.int32, gate.shape, 0)
        lane = lax.broadcasted_iota(jnp.int32, gate.shape, 1)
        rest = jnp.where(lane // cap == row, gate, F32(0.0))
        for i in range(3):
            piece = rest.astype(BF)
            rest = rest - piece.astype(F32)
            got = jnp.dot(piece, m_ref[...], preferred_element_type=F32)
            refs[-1][i * experts : (i + 1) * experts, :] = got.astype(BF)

    return pl.pallas_call(
        kernel,
        in_specs=[pl.BlockSpec(memory_space=pltpu.VMEM)] * 2 + [HBM] * len(after),
        out_specs=pl.BlockSpec(memory_space=pltpu.VMEM),
        out_shape=jax.ShapeDtypeStruct((3 * experts, match.shape[1]), BF),
    )(returned, match, *after)


def shards(out_grad, router_weight, down_weight, hidden_saved, slot_token, slot_count, slot_gate):
    grad = out_grad[0]
    tokens = slot_token[0, 0]
    counts = slot_count[0, 0]
    gates = slot_gate[0, 0]
    weight = down_weight[0]
    held = hidden_saved[0, 0]
    experts, capacity = tokens.shape
    tok_count, width = grad.shape
    me = lax.axis_index("expert")
    mx, mz = me // NZ, me % NZ
    where = jnp.stack([mx, mz]).astype(jnp.int32)

    where = jnp.concatenate([jnp.stack([mx, mz]).astype(jnp.int32), counts])

    with jax.named_scope("next_section"):
        grad_next = passed_along(grad, "section", -1)
        router_next = passed_along(router_weight[0].T, "section", -1)
        router_next = jnp.concatenate([router_next] * 3, 0)

    def exchanged(rows):
        with jax.named_scope("exchange_x"):
            return [rows[0]] + [lax.ppermute(rows[k], "expert", shift_x(k)) for k in range(1, NX)]

    last = NZ // 2
    order = [[0]] + [[NZ - t, t] for t in range(1, last)] + [[last]]
    with jax.named_scope("pick"):
        spread, *rows = begin(where, grad, tokens, gates)
        line = [[x * NZ + z for z in range(NZ)] for x in range(NX)]
        metas = lax.all_to_all(
            spread, "expert", split_axis=0, concat_axis=0, axis_index_groups=line, tiled=True
        )
    up = down = grad
    arrived, scaled, written = [exchanged(rows)], [], None
    for t in range(1, last + 1):
        with jax.named_scope("ring_z"):
            up = lax.ppermute(up, "expert", shift_z(1))
            down = lax.ppermute(down, "expert", shift_z(-1))
        with jax.named_scope("pick"):
            blocks = [[up], [down]] if t < last else [[up, down]]
            got = pick_rows(where, blocks, metas, order[t], scaled[t - 2 : t - 1], t == last - 1)
            rows = got[:NX]
            if t < last:
                up, down = hold(got[NX:] or [up, down], arrived[t - 1][1:] + [rows[0]])
            arrived.append(exchanged(rows))
        with jax.named_scope("project"):
            *written, piece = project(where, arrived[t - 1], weight, held, order[t - 1], written)
        scaled.append(piece)
    with jax.named_scope("project"):
        *written, piece = project(where, arrived[last], weight, held, order[last], written)
    scaled.append(piece)
    hidden_grad, partial = written

    with jax.named_scope("gate_return"):
        returned = lax.all_to_all(partial, "expert", split_axis=0, concat_axis=0, tiled=True)

    with jax.named_scope("weight_grad"):
        down_grad = weight_grad(where, [r for rows in arrived for r in rows], scaled, width)

    with jax.named_scope("input_grad"):
        slots = lax.broadcasted_iota(jnp.int32, (experts, capacity), 1)
        spot = jnp.where(slots < counts[:, None], tokens, -1).reshape(-1, 1)
        match = (spot == lax.broadcasted_iota(jnp.int32, (1, tok_count), 1)).astype(BF)
        logit_grad = logits(returned, match, [down_grad])
        logit_next = passed_along(logit_grad, "section", -1)
        passed = finish(where, grad_next, router_next, logit_next)
    return (down_grad[None], hidden_grad[None, None], passed[None])


def solution(mesh):
    return jax.shard_map(
        shards,
        mesh=mesh,
        in_specs=(
            P("section", "expert", None),
            P("section", None, None),
            P("section", "expert", None),
            P("section", "expert", None, None, None),
            P("section", "expert", None, None),
            P("section", "expert", None),
            P("section", "expert", None, None),
        ),
        out_specs=(
            P("section", "expert", None),
            P("section", "expert", None, None, None),
            P("section", "expert", None),
        ),
        check_vma=False,
    )
```

```python
import jax
import jax.numpy as jnp
from jax import lax
from jax.experimental import pallas as pl
from jax.experimental.pallas import tpu as pltpu
from jax.sharding import PartitionSpec as P

NX, NZ = 4, 8
TILE = 1792
WIDE = 1792
LANES = 128
META = 4
BF, F32 = jnp.bfloat16, jnp.float32


def shift_x(k):
    return [(x * NZ + z, (x + k) % NX * NZ + z) for x in range(NX) for z in range(NZ)]


def shift_z(k):
    return [(x * NZ + z, x * NZ + (z + k) % NZ) for x in range(NX) for z in range(NZ)]


def passed_along(value, axis, steps):
    count = lax.axis_size(axis)
    initial, last = (max(0, -steps), min(count, count - steps))
    return lax.ppermute(value, axis, [(source, source + steps) for source in range(initial, last)])


def call(kernel, grid, in_specs, out_specs, out_shape, scratch=(), aliases=None, flops=0, nbytes=0, vmem=63):
    return pl.pallas_call(
        kernel,
        grid_spec=pltpu.PrefetchScalarGridSpec(
            num_scalar_prefetch=1,
            grid=grid,
            in_specs=in_specs,
            out_specs=out_specs,
            scratch_shapes=list(scratch),
        ),
        out_shape=out_shape,
        input_output_aliases=aliases or {},
        compiler_params=pltpu.CompilerParams(vmem_limit_bytes=vmem * 1024 * 1024),
        cost_estimate=pl.CostEstimate(flops=flops, bytes_accessed=nbytes, transcendentals=0),
    )


def whole(shape):
    return pl.BlockSpec(shape, lambda j, w: (0,) * len(shape))


def columns(rows, tile, start):
    return pl.BlockSpec((rows, tile), lambda j, w: (0, j + start // tile))


HBM = pl.BlockSpec(memory_space=pl.ANY)


def picked(w_ref, meta, parts, outs, at_row):
    slots, tokens = meta.shape[0], parts[0].shape[0]
    cap = slots // NX
    half = w_ref[1] // (NZ // 2)
    lane = lax.broadcasted_iota(jnp.int32, (slots, LANES), 1)
    wanted = jnp.sum(jnp.where(lane == META * half, meta.astype(F32), F32(0.0)), axis=1, keepdims=True)
    place = lax.broadcasted_iota(jnp.int32, (slots, tokens), 1).astype(F32)
    hot = jnp.where(wanted == place, F32(1.0), F32(0.0)).astype(BF)
    at = 0
    for part in parts:
        got = jnp.dot(hot, part[...], preferred_element_type=F32).astype(BF)
        for k in range(NX):
            outs[k][at_row : at_row + cap, at : at + part.shape[1]] = got[k * cap : (k + 1) * cap]
        at += part.shape[1]
    for k in range(NX):
        outs[k][at_row : at_row + cap, at:] = meta[k * cap : (k + 1) * cap]


def begin(where, grad, tokens, gates):
    count, width = grad.shape
    cap = tokens.shape[1]

    def kernel(w_ref, g_ref, t_ref, s_ref, own_ref, meta_ref, out_ref):
        slot = lax.broadcasted_iota(jnp.int32, (1, cap), 1)
        for k in range(NX):
            lines = []
            for half in (0, 1):
                e = lax.rem(w_ref[0] + k, NX) * 2 + half
                live = slot < w_ref[2 + e]
                lines.append(jnp.where(live, t_ref[pl.ds(e, 1), :], -1).astype(F32))
                rest = jnp.where(live, s_ref[pl.ds(e, 1), :], F32(0.0))
                for _ in range(META - 1):
                    piece = rest.astype(BF).astype(F32)
                    lines.append(piece)
                    rest = rest - piece
            table = jnp.concatenate(lines, 0)
            table = jnp.concatenate([table, jnp.zeros((2 * META, LANES - cap), F32)], 1)
            table = jnp.concatenate([table, jnp.zeros((LANES - 2 * META, LANES), F32)], 0).T
            own_ref[0, k * cap : (k + 1) * cap, :] = table[:cap].astype(BF)
            for z in range(NZ):
                meta_ref[z, k * cap : (k + 1) * cap, :] = table[:cap].astype(BF)
        picked(w_ref, own_ref[0], [g_ref], [out_ref.at[lax.rem(w_ref[0] + k, NX)] for k in range(NX)], 0)

    full = width + LANES
    return call(
        kernel,
        (1,),
        [whole(x.shape) for x in (grad, tokens, gates)],
        [whole((n, NX * cap, LANES)) for n in (1, NZ)] + [whole((NX, cap, full))],
        [jax.ShapeDtypeStruct((n, NX * cap, LANES), BF) for n in (1, NZ)]
        + [jax.ShapeDtypeStruct((NX, cap, full), BF)],
        flops=2 * NX * cap * count * width,
        nbytes=6 * count * width,
    )(where, grad, tokens, gates)


def pick_rows(where, blocks, metas, places, after, cut):
    n = len(blocks)
    flat = [x for block in blocks for x in block]
    tokens = flat[0].shape[0]
    width = sum(x.shape[1] for x in blocks[0])
    slots = metas[0].shape[1]
    cap = slots // NX
    mid = width // 2
    cuts = 2 if cut else 0

    def kernel(w_ref, *refs):
        outs = refs[len(refs) - NX - cuts :]
        for b in range(n):
            parts = refs[b * len(blocks[b]) : (b + 1) * len(blocks[b])]
            picked(w_ref, refs[len(flat) + b][0], parts, outs[:NX], b * cap)
        if cut:
            outs[NX][...] = refs[0][:, :mid]
            outs[NX + 1][...] = refs[1][:, mid:]

    shapes = [(n * cap, width + LANES)] * NX + [(tokens, mid)] * cuts
    return call(
        kernel,
        (1,),
        [whole(x.shape) for x in flat]
        + [
            pl.BlockSpec((1, slots, LANES), lambda j, w, d=d: (0 if d is None else lax.rem(w[1] + d, NZ), 0, 0))
            for d in places
        ]
        + [HBM] * len(after),
        [whole(x) for x in shapes],
        [jax.ShapeDtypeStruct(x, BF) for x in shapes],
        flops=2 * n * slots * tokens * width,
        nbytes=4 * n * tokens * width,
    )(where, *flat, *metas, *after)


def hold(arrays, after):
    n = len(arrays)
    return pl.pallas_call(
        lambda *refs: None,
        in_specs=[HBM] * (n + len(after)),
        out_specs=[HBM] * n,
        out_shape=[jax.ShapeDtypeStruct(x.shape, x.dtype) for x in arrays],
        input_output_aliases={i: i for i in range(n)},
    )(*arrays, *after)


def project(where, got, weight, held, shifts, before):
    rows = got[0].shape[0]
    hid, width = weight.shape
    arrays = len(got)
    cap = rows * arrays // NX // len(shifts)
    steps = width // 2 // TILE
    n = NX * len(shifts)

    def kernel(w_ref, *refs):
        lows, highs, metas = refs[:arrays], refs[arrays : 2 * arrays], refs[2 * arrays : 3 * arrays]
        w_low, w_high, held_hbm = refs[3 * arrays : 3 * arrays + 3]
        hid_hbm, part_hbm, scaled_ref, acc, held_v, hid_v, part_v, sem_in, sem_hid, sem_part = refs[-10:]
        step = pl.program_id(0)

        def source(j):
            if arrays == 1:
                return j * NZ + w_ref[1]
            k, d = j // len(shifts), shifts[j % len(shifts)]
            return lax.rem(w_ref[0] + (NX - k), NX) * NZ + lax.rem(w_ref[1] + d, NZ)

        fetch = [pltpu.make_async_copy(held_hbm.at[source(j)], held_v.at[j], sem_in.at[j]) for j in range(n)]

        @pl.when(step == 0)
        def _():
            for copy in fetch:
                copy.start()

        contract = (((1,), (1,)), ((), ()))
        a = jnp.concatenate([r[...] for r in lows], 0)
        b = jnp.concatenate([r[...] for r in highs], 0)
        add = lax.dot_general(a, w_low[...], contract, preferred_element_type=F32)
        add += lax.dot_general(b, w_high[...], contract, preferred_element_type=F32)

        @pl.when(step == 0)
        def _():
            acc[...] = add

        @pl.when(step > 0)
        def _():
            acc[...] += add

        @pl.when(step == steps - 1)
        def _():
            half = w_ref[1] // (NZ // 2)
            lane = lax.broadcasted_iota(jnp.int32, (rows, LANES), 1) - META * half
            is_gate = (lane >= 1) & (lane < META)
            gate = jnp.concatenate(
                [
                    jnp.sum(jnp.where(is_gate, m[...].astype(F32), F32(0.0)), axis=1, keepdims=True)
                    for m in metas
                ],
                0,
            )
            proj = acc[...]
            hid_v[...] = (gate * proj).astype(BF).reshape(n, cap, hid)
            for copy in fetch:
                copy.wait()
            held_f = held_v[...].reshape(n * cap, hid).astype(F32)
            scaled_ref[...] = (held_f * gate).T.astype(BF)
            both = held_f * proj
            for j in range(n):
                part_v[j] = jnp.sum(both[j * cap : (j + 1) * cap].T, axis=0, keepdims=True)
            stores = []
            for j in range(n):
                stores.append(pltpu.make_async_copy(hid_v.at[j], hid_hbm.at[source(j)], sem_hid.at[j]))
                stores.append(pltpu.make_async_copy(part_v.at[j], part_hbm.at[source(j)], sem_part.at[j]))
            for copy in stores:
                copy.start()
            for copy in stores:
                copy.wait()

    extra = list(before) if before else []
    first = 1 + 3 * arrays + 3
    sources = held.shape[0]
    return call(
        kernel,
        (steps,),
        [columns(rows, TILE, 0)] * arrays
        + [columns(rows, TILE, width // 2)] * arrays
        + [pl.BlockSpec((rows, LANES), lambda j, w: (0, width // LANES))] * arrays
        + [columns(hid, TILE, 0), columns(hid, TILE, width // 2), HBM]
        + [HBM] * len(extra),
        [HBM, HBM, whole((hid, n * cap))],
        [
            jax.ShapeDtypeStruct(held.shape, BF),
            jax.ShapeDtypeStruct((sources, 1, cap), F32),
            jax.ShapeDtypeStruct((hid, n * cap), BF),
        ],
        [
            pltpu.VMEM((n * cap, hid), F32),
            pltpu.VMEM((n, cap, hid), BF),
            pltpu.VMEM((n, cap, hid), BF),
            pltpu.VMEM((n, 1, cap), F32),
            pltpu.SemaphoreType.DMA((n,)),
            pltpu.SemaphoreType.DMA((n,)),
            pltpu.SemaphoreType.DMA((n,)),
        ],
        {first: 0, first + 1: 1} if extra else {},
        flops=2 * n * cap * hid * width,
        nbytes=2 * width * (hid + n * cap),
    )(where, *got, *got, *got, weight, weight, held, *extra)


def weight_grad(where, rows, scaled, width):
    hid = scaled[0].shape[0]
    n, m = len(rows), len(scaled)
    total = sum(r.shape[0] for r in rows)

    def kernel(w_ref, *refs):
        b = jnp.concatenate([r[...] for r in refs[:n]], 0)
        a = jnp.concatenate([r[...] for r in refs[n : n + m]], 1)
        refs[-1][...] = jnp.dot(a, b, preferred_element_type=F32).astype(BF)

    return call(
        kernel,
        (width // WIDE,),
        [columns(r.shape[0], WIDE, 0) for r in rows] + [whole(x.shape) for x in scaled],
        columns(hid, WIDE, 0),
        jax.ShapeDtypeStruct((hid, width), BF),
        flops=2 * total * hid * width,
        nbytes=2 * width * (hid + total),
    )(where, *rows, *scaled)


def finish(where, grad, router, logit):
    rows, width = grad.shape

    def kernel(w_ref, g_ref, r_ref, l_ref, out_ref):
        piece = l_ref[...].astype(F32).T.astype(BF)
        add = jnp.dot(piece, r_ref[...], preferred_element_type=F32)
        out_ref[...] = (g_ref[...].astype(F32) + add).astype(BF)

    return call(
        kernel,
        (2,),
        [columns(rows, width // 2, 0), columns(router.shape[0], width // 2, 0), whole(logit.shape)],
        columns(rows, width // 2, 0),
        jax.ShapeDtypeStruct((rows, width), BF),
        flops=2 * rows * width * router.shape[0],
        nbytes=4 * rows * width,
        vmem=16,
    )(where, grad, router, logit)


def logits(returned, match, after):
    owners, _, cap = returned.shape
    experts = match.shape[0] // cap
    group = owners // experts

    def kernel(r_ref, m_ref, *refs):
        lines = []
        for e in range(experts):
            lines.append(sum(r_ref[e * group + q] for q in range(group)))
        gate = jnp.concatenate([jnp.concatenate(lines, 0)] * experts, 1)
        row = lax.broadcasted_iota(jnp.int32, gate.shape, 0)
        lane = lax.broadcasted_iota(jnp.int32, gate.shape, 1)
        rest = jnp.where(lane // cap == row, gate, F32(0.0))
        for i in range(3):
            piece = rest.astype(BF)
            rest = rest - piece.astype(F32)
            got = jnp.dot(piece, m_ref[...], preferred_element_type=F32)
            refs[-1][i * experts : (i + 1) * experts, :] = got.astype(BF)

    return pl.pallas_call(
        kernel,
        in_specs=[pl.BlockSpec(memory_space=pltpu.VMEM)] * 2 + [HBM] * len(after),
        out_specs=pl.BlockSpec(memory_space=pltpu.VMEM),
        out_shape=jax.ShapeDtypeStruct((3 * experts, match.shape[1]), BF),
    )(returned, match, *after)


def shards(out_grad, router_weight, down_weight, hidden_saved, slot_token, slot_count, slot_gate):
    grad = out_grad[0]
    tokens = slot_token[0, 0]
    counts = slot_count[0, 0]
    gates = slot_gate[0, 0]
    weight = down_weight[0]
    held = hidden_saved[0, 0]
    experts, capacity = tokens.shape
    tok_count, width = grad.shape
    me = lax.axis_index("expert")
    mx, mz = me // NZ, me % NZ
    where = jnp.stack([mx, mz]).astype(jnp.int32)

    where = jnp.concatenate([jnp.stack([mx, mz]).astype(jnp.int32), counts])

    with jax.named_scope("next_section"):
        grad_next = passed_along(grad, "section", -1)
        router_next = passed_along(router_weight[0].T, "section", -1)
        router_next = jnp.concatenate([router_next] * 3, 0)

    def exchanged(rows):
        with jax.named_scope("exchange_x"):
            return [rows[0]] + [lax.ppermute(rows[k], "expert", shift_x(k)) for k in range(1, NX)]

    last = NZ // 2
    order = [[0]] + [[NZ - t, t] for t in range(1, last)] + [[last]]
    with jax.named_scope("pick"):
        own, spread, rows = begin(where, grad, tokens, gates)
        near = [lax.ppermute(own, "expert", shift_z(k)) for k in (1, -1)]
        line = [[x * NZ + z for z in range(NZ)] for x in range(NX)]
        metas = lax.all_to_all(
            spread, "expert", split_axis=0, concat_axis=0, axis_index_groups=line, tiled=True
        )
    up = down = grad
    with jax.named_scope("exchange_x"):
        across = [[x * NZ + z for x in range(NX)] for z in range(NZ)]
        rows = lax.all_to_all(
            rows, "expert", split_axis=0, concat_axis=0, axis_index_groups=across, tiled=True
        )
    arrived, scaled, written = [[rows.reshape(-1, rows.shape[2])]], [], None
    for t in range(1, last + 1):
        with jax.named_scope("ring_z"):
            up = lax.ppermute(up, "expert", shift_z(1))
            down = lax.ppermute(down, "expert", shift_z(-1))
        with jax.named_scope("pick"):
            blocks = [[up], [down]] if t < last else [[up, down]]
            tables, places = (near, [None, None]) if t == 1 else ([metas] * len(blocks), order[t])
            got = pick_rows(where, blocks, tables, places, scaled[t - 2 : t - 1], t == last - 1)
            rows = got[:NX]
            if t < last:
                up, down = hold(got[NX:] or [up, down], arrived[t - 1][-3:] + [rows[0]])
            arrived.append(exchanged(rows))
        with jax.named_scope("project"):
            *written, piece = project(where, arrived[t - 1], weight, held, order[t - 1], written)
        scaled.append(piece)
    with jax.named_scope("project"):
        *written, piece = project(where, arrived[last], weight, held, order[last], written)
    scaled.append(piece)
    hidden_grad, partial = written

    with jax.named_scope("gate_return"):
        returned = lax.all_to_all(partial, "expert", split_axis=0, concat_axis=0, tiled=True)

    with jax.named_scope("weight_grad"):
        down_grad = weight_grad(where, [r for rows in arrived for r in rows], scaled, width)

    with jax.named_scope("input_grad"):
        slots = lax.broadcasted_iota(jnp.int32, (experts, capacity), 1)
        spot = jnp.where(slots < counts[:, None], tokens, -1).reshape(-1, 1)
        match = (spot == lax.broadcasted_iota(jnp.int32, (1, tok_count), 1)).astype(BF)
        logit_grad = logits(returned, match, [down_grad])
        logit_next = passed_along(logit_grad, "section", -1)
        passed = finish(where, grad_next, router_next, logit_next)
    return (down_grad[None], hidden_grad[None, None], passed[None])


def solution(mesh):
    return jax.shard_map(
        shards,
        mesh=mesh,
        in_specs=(
            P("section", "expert", None),
            P("section", None, None),
            P("section", "expert", None),
            P("section", "expert", None, None, None),
            P("section", "expert", None, None),
            P("section", "expert", None),
            P("section", "expert", None, None),
        ),
        out_specs=(
            P("section", "expert", None),
            P("section", "expert", None, None, None),
            P("section", "expert", None),
        ),
        check_vma=False,
    )
```

```python
import jax
import jax.numpy as jnp
from jax import lax
from jax.experimental import pallas as pl
from jax.experimental.pallas import tpu as pltpu
from jax.sharding import PartitionSpec as P

NX, NZ = 4, 8
TILE = 1792
WIDE = 1792
LANES = 128
META = 4
BF, F32 = jnp.bfloat16, jnp.float32


def shift_x(k):
    return [(x * NZ + z, (x + k) % NX * NZ + z) for x in range(NX) for z in range(NZ)]


def shift_z(k):
    return [(x * NZ + z, x * NZ + (z + k) % NZ) for x in range(NX) for z in range(NZ)]


def passed_along(value, axis, steps):
    count = lax.axis_size(axis)
    initial, last = (max(0, -steps), min(count, count - steps))
    return lax.ppermute(value, axis, [(source, source + steps) for source in range(initial, last)])


def call(kernel, grid, in_specs, out_specs, out_shape, scratch=(), aliases=None, flops=0, nbytes=0, vmem=63):
    return pl.pallas_call(
        kernel,
        grid_spec=pltpu.PrefetchScalarGridSpec(
            num_scalar_prefetch=1,
            grid=grid,
            in_specs=in_specs,
            out_specs=out_specs,
            scratch_shapes=list(scratch),
        ),
        out_shape=out_shape,
        input_output_aliases=aliases or {},
        compiler_params=pltpu.CompilerParams(vmem_limit_bytes=vmem * 1024 * 1024),
        cost_estimate=pl.CostEstimate(flops=flops, bytes_accessed=nbytes, transcendentals=0),
    )


def whole(shape):
    return pl.BlockSpec(shape, lambda j, w: (0,) * len(shape))


def columns(rows, tile, start):
    return pl.BlockSpec((rows, tile), lambda j, w: (0, j + start // tile))


HBM = pl.BlockSpec(memory_space=pl.ANY)


def picked(w_ref, meta, parts, outs, at_row):
    slots, tokens = meta.shape[0], parts[0].shape[0]
    cap = slots // NX
    half = w_ref[1] // (NZ // 2)
    lane = lax.broadcasted_iota(jnp.int32, (slots, LANES), 1)
    wanted = jnp.sum(jnp.where(lane == META * half, meta.astype(F32), F32(0.0)), axis=1, keepdims=True)
    place = lax.broadcasted_iota(jnp.int32, (slots, tokens), 1).astype(F32)
    hot = jnp.where(wanted == place, F32(1.0), F32(0.0)).astype(BF)
    at = 0
    for part in parts:
        got = jnp.dot(hot, part[...], preferred_element_type=F32).astype(BF)
        for k in range(NX):
            outs[k][at_row : at_row + cap, at : at + part.shape[1]] = got[k * cap : (k + 1) * cap]
        at += part.shape[1]
    for k in range(NX):
        outs[k][at_row : at_row + cap, at:] = meta[k * cap : (k + 1) * cap]


def begin(where, grad, tokens, gates):
    count, width = grad.shape
    cap = tokens.shape[1]

    def kernel(w_ref, g_ref, t_ref, s_ref, own_ref, out_ref):
        slot = lax.broadcasted_iota(jnp.int32, (1, cap), 1)
        for k in range(NX):
            lines = []
            for half in (0, 1):
                e = lax.rem(w_ref[0] + k, NX) * 2 + half
                live = slot < w_ref[2 + e]
                lines.append(jnp.where(live, t_ref[pl.ds(e, 1), :], -1).astype(F32))
                rest = jnp.where(live, s_ref[pl.ds(e, 1), :], F32(0.0))
                for _ in range(META - 1):
                    piece = rest.astype(BF).astype(F32)
                    lines.append(piece)
                    rest = rest - piece
            table = jnp.concatenate(lines, 0)
            table = jnp.concatenate([table, jnp.zeros((2 * META, LANES - cap), F32)], 1)
            table = jnp.concatenate([table, jnp.zeros((LANES - 2 * META, LANES), F32)], 0).T
            own_ref[0, k * cap : (k + 1) * cap, :] = table[:cap].astype(BF)
        picked(w_ref, own_ref[0], [g_ref], [out_ref.at[lax.rem(w_ref[0] + k, NX)] for k in range(NX)], 0)

    full = width + LANES
    return call(
        kernel,
        (1,),
        [whole(x.shape) for x in (grad, tokens, gates)],
        [whole((1, NX * cap, LANES)), whole((NX, cap, full))],
        [jax.ShapeDtypeStruct((1, NX * cap, LANES), BF), jax.ShapeDtypeStruct((NX, cap, full), BF)],
        flops=2 * NX * cap * count * width,
        nbytes=6 * count * width,
    )(where, grad, tokens, gates)


def pick_rows(where, blocks, tables, after, cut):
    n = len(blocks)
    flat = [x for block in blocks for x in block]
    tokens = flat[0].shape[0]
    full = sum(x.shape[1] for x in blocks[0]) + (LANES if tables else 0)
    width = full - LANES
    cap = tokens // NX
    mid = width // 2

    def kernel(w_ref, *refs):
        outs = refs[len(refs) - len(shapes) :]
        for b in range(n):
            parts = list(refs[b * len(blocks[b]) : (b + 1) * len(blocks[b])])
            if tables:
                meta = refs[len(flat) + b][0]
                outs[NX + b][:, :width] = parts[0][...]
                outs[NX + b][:, width:] = meta
            else:
                own = parts[-1].shape[1] - LANES
                meta = parts[-1][:, own:]
                parts[-1] = parts[-1].at[:, :own]
            picked(w_ref, meta, parts, outs[:NX], b * cap)
        if cut:
            outs[NX][...] = refs[0][:, :mid]
            outs[NX + 1][...] = refs[1][:, mid:]

    shapes = [(n * cap, full)] * NX
    if tables:
        shapes += [(tokens, full)] * n
    if cut:
        shapes += [(tokens, mid), (tokens, full - mid)]
    return call(
        kernel,
        (1,),
        [whole(x.shape) for x in flat + tables] + [HBM] * len(after),
        [whole(x) for x in shapes],
        [jax.ShapeDtypeStruct(x, BF) for x in shapes],
        flops=2 * n * tokens * tokens * width,
        nbytes=4 * n * tokens * width,
    )(where, *flat, *tables, *after)


def hold(arrays, after):
    n = len(arrays)
    return pl.pallas_call(
        lambda *refs: None,
        in_specs=[HBM] * (n + len(after)),
        out_specs=[HBM] * n,
        out_shape=[jax.ShapeDtypeStruct(x.shape, x.dtype) for x in arrays],
        input_output_aliases={i: i for i in range(n)},
    )(*arrays, *after)


def project(where, got, weight, held, shifts, before):
    rows = got[0].shape[0]
    hid, width = weight.shape
    arrays = len(got)
    cap = rows * arrays // NX // len(shifts)
    steps = width // 2 // TILE
    n = NX * len(shifts)

    def kernel(w_ref, *refs):
        lows, highs, metas = refs[:arrays], refs[arrays : 2 * arrays], refs[2 * arrays : 3 * arrays]
        w_low, w_high, held_hbm = refs[3 * arrays : 3 * arrays + 3]
        hid_hbm, part_hbm, scaled_ref, acc, held_v, hid_v, part_v, sem_in, sem_hid, sem_part = refs[-10:]
        step = pl.program_id(0)

        def source(j):
            if arrays == 1:
                return j * NZ + w_ref[1]
            k, d = j // len(shifts), shifts[j % len(shifts)]
            return lax.rem(w_ref[0] + (NX - k), NX) * NZ + lax.rem(w_ref[1] + d, NZ)

        fetch = [pltpu.make_async_copy(held_hbm.at[source(j)], held_v.at[j], sem_in.at[j]) for j in range(n)]

        @pl.when(step == 0)
        def _():
            for copy in fetch:
                copy.start()

        contract = (((1,), (1,)), ((), ()))
        a = jnp.concatenate([r[...] for r in lows], 0)
        b = jnp.concatenate([r[...] for r in highs], 0)
        add = lax.dot_general(a, w_low[...], contract, preferred_element_type=F32)
        add += lax.dot_general(b, w_high[...], contract, preferred_element_type=F32)

        @pl.when(step == 0)
        def _():
            acc[...] = add

        @pl.when(step > 0)
        def _():
            acc[...] += add

        @pl.when(step == steps - 1)
        def _():
            half = w_ref[1] // (NZ // 2)
            lane = lax.broadcasted_iota(jnp.int32, (rows, LANES), 1) - META * half
            is_gate = (lane >= 1) & (lane < META)
            gate = jnp.concatenate(
                [
                    jnp.sum(jnp.where(is_gate, m[...].astype(F32), F32(0.0)), axis=1, keepdims=True)
                    for m in metas
                ],
                0,
            )
            proj = acc[...]
            hid_v[...] = (gate * proj).astype(BF).reshape(n, cap, hid)
            for copy in fetch:
                copy.wait()
            held_f = held_v[...].reshape(n * cap, hid).astype(F32)
            scaled_ref[...] = (held_f * gate).T.astype(BF)
            both = held_f * proj
            for j in range(n):
                part_v[j] = jnp.sum(both[j * cap : (j + 1) * cap].T, axis=0, keepdims=True)
            stores = []
            for j in range(n):
                stores.append(pltpu.make_async_copy(hid_v.at[j], hid_hbm.at[source(j)], sem_hid.at[j]))
                stores.append(pltpu.make_async_copy(part_v.at[j], part_hbm.at[source(j)], sem_part.at[j]))
            for copy in stores:
                copy.start()
            for copy in stores:
                copy.wait()

    extra = list(before) if before else []
    first = 1 + 3 * arrays + 3
    sources = held.shape[0]
    return call(
        kernel,
        (steps,),
        [columns(rows, TILE, 0)] * arrays
        + [columns(rows, TILE, width // 2)] * arrays
        + [pl.BlockSpec((rows, LANES), lambda j, w: (0, width // LANES))] * arrays
        + [columns(hid, TILE, 0), columns(hid, TILE, width // 2), HBM]
        + [HBM] * len(extra),
        [HBM, HBM, whole((hid, n * cap))],
        [
            jax.ShapeDtypeStruct(held.shape, BF),
            jax.ShapeDtypeStruct((sources, 1, cap), F32),
            jax.ShapeDtypeStruct((hid, n * cap), BF),
        ],
        [
            pltpu.VMEM((n * cap, hid), F32),
            pltpu.VMEM((n, cap, hid), BF),
            pltpu.VMEM((n, cap, hid), BF),
            pltpu.VMEM((n, 1, cap), F32),
            pltpu.SemaphoreType.DMA((n,)),
            pltpu.SemaphoreType.DMA((n,)),
            pltpu.SemaphoreType.DMA((n,)),
        ],
        {first: 0, first + 1: 1} if extra else {},
        flops=2 * n * cap * hid * width,
        nbytes=2 * width * (hid + n * cap),
    )(where, *got, *got, *got, weight, weight, held, *extra)


def weight_grad(where, rows, scaled, width):
    hid = scaled[0].shape[0]
    n, m = len(rows), len(scaled)
    total = sum(r.shape[0] for r in rows)

    def kernel(w_ref, *refs):
        b = jnp.concatenate([r[...] for r in refs[:n]], 0)
        a = jnp.concatenate([r[...] for r in refs[n : n + m]], 1)
        refs[-1][...] = jnp.dot(a, b, preferred_element_type=F32).astype(BF)

    return call(
        kernel,
        (width // WIDE,),
        [columns(r.shape[0], WIDE, 0) for r in rows] + [whole(x.shape) for x in scaled],
        columns(hid, WIDE, 0),
        jax.ShapeDtypeStruct((hid, width), BF),
        flops=2 * total * hid * width,
        nbytes=2 * width * (hid + total),
    )(where, *rows, *scaled)


def finish(where, grad, router, logit):
    rows, width = grad.shape

    def kernel(w_ref, g_ref, r_ref, l_ref, out_ref):
        piece = l_ref[...].astype(F32).T.astype(BF)
        add = jnp.dot(piece, r_ref[...], preferred_element_type=F32)
        out_ref[...] = (g_ref[...].astype(F32) + add).astype(BF)

    return call(
        kernel,
        (2,),
        [columns(rows, width // 2, 0), columns(router.shape[0], width // 2, 0), whole(logit.shape)],
        columns(rows, width // 2, 0),
        jax.ShapeDtypeStruct((rows, width), BF),
        flops=2 * rows * width * router.shape[0],
        nbytes=4 * rows * width,
        vmem=16,
    )(where, grad, router, logit)


def logits(returned, match, after):
    owners, _, cap = returned.shape
    experts = match.shape[0] // cap
    group = owners // experts

    def kernel(r_ref, m_ref, *refs):
        lines = []
        for e in range(experts):
            lines.append(sum(r_ref[e * group + q] for q in range(group)))
        gate = jnp.concatenate([jnp.concatenate(lines, 0)] * experts, 1)
        row = lax.broadcasted_iota(jnp.int32, gate.shape, 0)
        lane = lax.broadcasted_iota(jnp.int32, gate.shape, 1)
        rest = jnp.where(lane // cap == row, gate, F32(0.0))
        for i in range(3):
            piece = rest.astype(BF)
            rest = rest - piece.astype(F32)
            got = jnp.dot(piece, m_ref[...], preferred_element_type=F32)
            refs[-1][i * experts : (i + 1) * experts, :] = got.astype(BF)

    return pl.pallas_call(
        kernel,
        in_specs=[pl.BlockSpec(memory_space=pltpu.VMEM)] * 2 + [HBM] * len(after),
        out_specs=pl.BlockSpec(memory_space=pltpu.VMEM),
        out_shape=jax.ShapeDtypeStruct((3 * experts, match.shape[1]), BF),
    )(returned, match, *after)


def shards(out_grad, router_weight, down_weight, hidden_saved, slot_token, slot_count, slot_gate):
    grad = out_grad[0]
    tokens = slot_token[0, 0]
    counts = slot_count[0, 0]
    gates = slot_gate[0, 0]
    weight = down_weight[0]
    held = hidden_saved[0, 0]
    experts, capacity = tokens.shape
    tok_count, width = grad.shape
    me = lax.axis_index("expert")
    mx, mz = me // NZ, me % NZ
    where = jnp.stack([mx, mz]).astype(jnp.int32)

    where = jnp.concatenate([jnp.stack([mx, mz]).astype(jnp.int32), counts])

    with jax.named_scope("next_section"):
        grad_next = passed_along(grad, "section", -1)
        router_next = passed_along(router_weight[0].T, "section", -1)
        router_next = jnp.concatenate([router_next] * 3, 0)

    def exchanged(rows):
        with jax.named_scope("exchange_x"):
            return [rows[0]] + [lax.ppermute(rows[k], "expert", shift_x(k)) for k in range(1, NX)]

    last = NZ // 2
    order = [[0]] + [[NZ - t, t] for t in range(1, last)] + [[last]]
    with jax.named_scope("pick"):
        own, rows = begin(where, grad, tokens, gates)
        near = [lax.ppermute(own, "expert", shift_z(k)) for k in (1, -1)]
    up = down = grad
    with jax.named_scope("exchange_x"):
        across = [[x * NZ + z for x in range(NX)] for z in range(NZ)]
        rows = lax.all_to_all(
            rows, "expert", split_axis=0, concat_axis=0, axis_index_groups=across, tiled=True
        )
    arrived, scaled, written = [[rows.reshape(-1, rows.shape[2])]], [], None
    for t in range(1, last + 1):
        with jax.named_scope("ring_z"):
            up = lax.ppermute(up, "expert", shift_z(1))
            down = lax.ppermute(down, "expert", shift_z(-1))
        with jax.named_scope("pick"):
            blocks = [[up], [down]] if t < last else [[up, down]]
            got = pick_rows(where, blocks, near if t == 1 else [], scaled[t - 2 : t - 1], t == last - 1)
            rows = got[:NX]
            if t < last:
                up, down = hold(got[NX:] or [up, down], arrived[t - 1][-3:] + [rows[0]])
            arrived.append(exchanged(rows))
        with jax.named_scope("project"):
            *written, piece = project(where, arrived[t - 1], weight, held, order[t - 1], written)
        scaled.append(piece)
    with jax.named_scope("project"):
        *written, piece = project(where, arrived[last], weight, held, order[last], written)
    scaled.append(piece)
    hidden_grad, partial = written

    with jax.named_scope("gate_return"):
        returned = lax.all_to_all(partial, "expert", split_axis=0, concat_axis=0, tiled=True)

    with jax.named_scope("weight_grad"):
        down_grad = weight_grad(where, [r for rows in arrived for r in rows], scaled, width)

    with jax.named_scope("input_grad"):
        slots = lax.broadcasted_iota(jnp.int32, (experts, capacity), 1)
        spot = jnp.where(slots < counts[:, None], tokens, -1).reshape(-1, 1)
        match = (spot == lax.broadcasted_iota(jnp.int32, (1, tok_count), 1)).astype(BF)
        logit_grad = logits(returned, match, [down_grad])
        logit_next = passed_along(logit_grad, "section", -1)
        passed = finish(where, grad_next, router_next, logit_next)
    return (down_grad[None], hidden_grad[None, None], passed[None])


def solution(mesh):
    return jax.shard_map(
        shards,
        mesh=mesh,
        in_specs=(
            P("section", "expert", None),
            P("section", None, None),
            P("section", "expert", None),
            P("section", "expert", None, None, None),
            P("section", "expert", None, None),
            P("section", "expert", None),
            P("section", "expert", None, None),
        ),
        out_specs=(
            P("section", "expert", None),
            P("section", "expert", None, None, None),
            P("section", "expert", None),
        ),
        check_vma=False,
    )
```

```python
import jax
import jax.numpy as jnp
from jax import lax
from jax.experimental import pallas as pl
from jax.experimental.pallas import tpu as pltpu
from jax.sharding import PartitionSpec as P

NX, NZ = 4, 8
TILE = 1792
WIDE = 1792
LANES = 128
META = 4
BF, F32 = jnp.bfloat16, jnp.float32


def shift_x(k):
    return [(x * NZ + z, (x + k) % NX * NZ + z) for x in range(NX) for z in range(NZ)]


def shift_z(k):
    return [(x * NZ + z, x * NZ + (z + k) % NZ) for x in range(NX) for z in range(NZ)]


def passed_along(value, axis, steps):
    count = lax.axis_size(axis)
    initial, last = (max(0, -steps), min(count, count - steps))
    return lax.ppermute(value, axis, [(source, source + steps) for source in range(initial, last)])


def call(kernel, grid, in_specs, out_specs, out_shape, scratch=(), aliases=None, flops=0, nbytes=0, vmem=64):
    return pl.pallas_call(
        kernel,
        grid_spec=pltpu.PrefetchScalarGridSpec(
            num_scalar_prefetch=1,
            grid=grid,
            in_specs=in_specs,
            out_specs=out_specs,
            scratch_shapes=list(scratch),
        ),
        out_shape=out_shape,
        input_output_aliases=aliases or {},
        compiler_params=pltpu.CompilerParams(vmem_limit_bytes=vmem * 1024 * 1024),
        cost_estimate=pl.CostEstimate(flops=flops, bytes_accessed=nbytes, transcendentals=0),
    )


def whole(shape):
    return pl.BlockSpec(shape, lambda j, w: (0,) * len(shape))


def columns(rows, tile, start):
    return pl.BlockSpec((rows, tile), lambda j, w: (0, j + start // tile))


HBM = pl.BlockSpec(memory_space=pl.ANY)


def picked(w_ref, meta, parts, outs, at_row):
    slots, tokens = meta.shape[0], parts[0].shape[0]
    cap = slots // NX
    half = w_ref[1] // (NZ // 2)
    lane = lax.broadcasted_iota(jnp.int32, (slots, LANES), 1)
    wanted = jnp.sum(jnp.where(lane == META * half, meta.astype(F32), F32(0.0)), axis=1, keepdims=True)
    place = lax.broadcasted_iota(jnp.int32, (slots, tokens), 1).astype(F32)
    hot = jnp.where(wanted == place, F32(1.0), F32(0.0)).astype(BF)
    at = 0
    for part in parts:
        got = jnp.dot(hot, part[...], preferred_element_type=F32).astype(BF)
        for k in range(NX):
            outs[k][at_row : at_row + cap, at : at + part.shape[1]] = got[k * cap : (k + 1) * cap]
        at += part.shape[1]
    for k in range(NX):
        outs[k][at_row : at_row + cap, at:] = meta[k * cap : (k + 1) * cap]


def begin(where, grad, tokens, gates):
    count, width = grad.shape
    cap = tokens.shape[1]

    def kernel(w_ref, g_ref, t_ref, s_ref, own_ref, out_ref):
        slot = lax.broadcasted_iota(jnp.int32, (1, cap), 1)
        for k in range(NX):
            lines = []
            for half in (0, 1):
                e = lax.rem(w_ref[0] + k, NX) * 2 + half
                live = slot < w_ref[2 + e]
                lines.append(jnp.where(live, t_ref[pl.ds(e, 1), :], -1).astype(F32))
                rest = jnp.where(live, s_ref[pl.ds(e, 1), :], F32(0.0))
                for _ in range(META - 1):
                    piece = rest.astype(BF).astype(F32)
                    lines.append(piece)
                    rest = rest - piece
            table = jnp.concatenate(lines, 0)
            table = jnp.concatenate([table, jnp.zeros((2 * META, LANES - cap), F32)], 1)
            table = jnp.concatenate([table, jnp.zeros((LANES - 2 * META, LANES), F32)], 0).T
            own_ref[0, k * cap : (k + 1) * cap, :] = table[:cap].astype(BF)
        picked(w_ref, own_ref[0], [g_ref], [out_ref.at[lax.rem(w_ref[0] + k, NX)] for k in range(NX)], 0)

    full = width + LANES
    return call(
        kernel,
        (1,),
        [whole(x.shape) for x in (grad, tokens, gates)],
        [whole((1, NX * cap, LANES)), whole((NX, cap, full))],
        [jax.ShapeDtypeStruct((1, NX * cap, LANES), BF), jax.ShapeDtypeStruct((NX, cap, full), BF)],
        flops=2 * NX * cap * count * width,
        nbytes=6 * count * width,
    )(where, grad, tokens, gates)


def pick_rows(where, blocks, tables, after, cut):
    n = len(blocks)
    flat = [x for block in blocks for x in block]
    tokens = flat[0].shape[0]
    full = sum(x.shape[1] for x in blocks[0]) + (LANES if tables else 0)
    width = full - LANES
    cap = tokens // NX
    mid = width // 2

    def kernel(w_ref, *refs):
        outs = refs[len(refs) - len(shapes) :]
        for b in range(n):
            parts = list(refs[b * len(blocks[b]) : (b + 1) * len(blocks[b])])
            if tables:
                meta = refs[len(flat) + b][0]
                outs[NX + b][:, :width] = parts[0][...]
                outs[NX + b][:, width:] = meta
            else:
                own = parts[-1].shape[1] - LANES
                meta = parts[-1][:, own:]
                parts[-1] = parts[-1].at[:, :own]
            picked(w_ref, meta, parts, outs[:NX], b * cap)
        if cut:
            outs[NX][...] = refs[0][:, :mid]
            outs[NX + 1][...] = refs[1][:, mid:]

    shapes = [(n * cap, full)] * NX
    if tables:
        shapes += [(tokens, full)] * n
    if cut:
        shapes += [(tokens, mid), (tokens, full - mid)]
    return call(
        kernel,
        (1,),
        [whole(x.shape) for x in flat + tables] + [HBM] * len(after),
        [whole(x) for x in shapes],
        [jax.ShapeDtypeStruct(x, BF) for x in shapes],
        flops=2 * n * tokens * tokens * width,
        nbytes=4 * n * tokens * width,
    )(where, *flat, *tables, *after)


def hold(arrays, after):
    n = len(arrays)
    return pl.pallas_call(
        lambda *refs: None,
        in_specs=[HBM] * (n + len(after)),
        out_specs=[HBM] * n,
        out_shape=[jax.ShapeDtypeStruct(x.shape, x.dtype) for x in arrays],
        input_output_aliases={i: i for i in range(n)},
    )(*arrays, *after)


def project(where, got, weight, held, shifts, before):
    rows = got[0].shape[0]
    hid, width = weight.shape
    arrays = len(got)
    cap = rows * arrays // NX // len(shifts)
    steps = width // 2 // TILE
    n = NX * len(shifts)

    def kernel(w_ref, *refs):
        lows, highs, metas = refs[:arrays], refs[arrays : 2 * arrays], refs[2 * arrays : 3 * arrays]
        w_low, w_high, held_hbm = refs[3 * arrays : 3 * arrays + 3]
        hid_hbm, part_hbm, scaled_ref, acc, held_v, hid_v, part_v, sem_in, sem_hid, sem_part = refs[-10:]
        step = pl.program_id(0)

        def source(j):
            if arrays == 1:
                return j * NZ + w_ref[1]
            k, d = j // len(shifts), shifts[j % len(shifts)]
            return lax.rem(w_ref[0] + (NX - k), NX) * NZ + lax.rem(w_ref[1] + d, NZ)

        fetch = [pltpu.make_async_copy(held_hbm.at[source(j)], held_v.at[j], sem_in.at[j]) for j in range(n)]

        @pl.when(step == 0)
        def _():
            for copy in fetch:
                copy.start()

        contract = (((1,), (1,)), ((), ()))
        a = jnp.concatenate([r[...] for r in lows], 0)
        b = jnp.concatenate([r[...] for r in highs], 0)
        add = lax.dot_general(a, w_low[...], contract, preferred_element_type=F32)
        add += lax.dot_general(b, w_high[...], contract, preferred_element_type=F32)

        @pl.when(step == 0)
        def _():
            acc[...] = add

        @pl.when(step > 0)
        def _():
            acc[...] += add

        @pl.when(step == steps - 1)
        def _():
            half = w_ref[1] // (NZ // 2)
            lane = lax.broadcasted_iota(jnp.int32, (rows, LANES), 1) - META * half
            is_gate = (lane >= 1) & (lane < META)
            gate = jnp.concatenate(
                [
                    jnp.sum(jnp.where(is_gate, m[...].astype(F32), F32(0.0)), axis=1, keepdims=True)
                    for m in metas
                ],
                0,
            )
            proj = acc[...]
            hid_v[...] = (gate * proj).astype(BF).reshape(n, cap, hid)
            for copy in fetch:
                copy.wait()
            held_f = held_v[...].reshape(n * cap, hid).astype(F32)
            scaled_ref[...] = (held_f * gate).T.astype(BF)
            both = held_f * proj
            for j in range(n):
                part_v[j] = jnp.sum(both[j * cap : (j + 1) * cap].T, axis=0, keepdims=True)
            stores = []
            for j in range(n):
                stores.append(pltpu.make_async_copy(hid_v.at[j], hid_hbm.at[source(j)], sem_hid.at[j]))
                stores.append(pltpu.make_async_copy(part_v.at[j], part_hbm.at[source(j)], sem_part.at[j]))
            for copy in stores:
                copy.start()
            for copy in stores:
                copy.wait()

    extra = list(before) if before else []
    first = 1 + 3 * arrays + 3
    sources = held.shape[0]
    return call(
        kernel,
        (steps,),
        [columns(rows, TILE, 0)] * arrays
        + [columns(rows, TILE, width // 2)] * arrays
        + [pl.BlockSpec((rows, LANES), lambda j, w: (0, width // LANES))] * arrays
        + [columns(hid, TILE, 0), columns(hid, TILE, width // 2), HBM]
        + [HBM] * len(extra),
        [HBM, HBM, whole((hid, n * cap))],
        [
            jax.ShapeDtypeStruct(held.shape, BF),
            jax.ShapeDtypeStruct((sources, 1, cap), F32),
            jax.ShapeDtypeStruct((hid, n * cap), BF),
        ],
        [
            pltpu.VMEM((n * cap, hid), F32),
            pltpu.VMEM((n, cap, hid), BF),
            pltpu.VMEM((n, cap, hid), BF),
            pltpu.VMEM((n, 1, cap), F32),
            pltpu.SemaphoreType.DMA((n,)),
            pltpu.SemaphoreType.DMA((n,)),
            pltpu.SemaphoreType.DMA((n,)),
        ],
        {first: 0, first + 1: 1} if extra else {},
        flops=2 * n * cap * hid * width,
        nbytes=2 * width * (hid + n * cap),
    )(where, *got, *got, *got, weight, weight, held, *extra)


def weight_grad(where, rows, scaled, width):
    hid = scaled[0].shape[0]
    n, m = len(rows), len(scaled)
    total = sum(r.shape[0] for r in rows)

    def kernel(w_ref, *refs):
        b = jnp.concatenate([r[...] for r in refs[:n]], 0)
        a = jnp.concatenate([r[...] for r in refs[n : n + m]], 1)
        refs[-1][...] = jnp.dot(a, b, preferred_element_type=F32).astype(BF)

    return call(
        kernel,
        (width // WIDE,),
        [columns(r.shape[0], WIDE, 0) for r in rows] + [whole(x.shape) for x in scaled],
        columns(hid, WIDE, 0),
        jax.ShapeDtypeStruct((hid, width), BF),
        flops=2 * total * hid * width,
        nbytes=2 * width * (hid + total),
    )(where, *rows, *scaled)


def finish(where, grad, router, logit):
    rows, width = grad.shape

    def kernel(w_ref, g_ref, r_ref, l_ref, out_ref):
        piece = l_ref[...].astype(F32).T.astype(BF)
        add = jnp.dot(piece, r_ref[...], preferred_element_type=F32)
        out_ref[...] = (g_ref[...].astype(F32) + add).astype(BF)

    return call(
        kernel,
        (2,),
        [columns(rows, width // 2, 0), columns(router.shape[0], width // 2, 0), whole(logit.shape)],
        columns(rows, width // 2, 0),
        jax.ShapeDtypeStruct((rows, width), BF),
        flops=2 * rows * width * router.shape[0],
        nbytes=4 * rows * width,
        vmem=16,
    )(where, grad, router, logit)


def logits(returned, match, after):
    owners, _, cap = returned.shape
    experts = match.shape[0] // cap
    group = owners // experts

    def kernel(r_ref, m_ref, *refs):
        lines = []
        for e in range(experts):
            lines.append(sum(r_ref[e * group + q] for q in range(group)))
        gate = jnp.concatenate([jnp.concatenate(lines, 0)] * experts, 1)
        row = lax.broadcasted_iota(jnp.int32, gate.shape, 0)
        lane = lax.broadcasted_iota(jnp.int32, gate.shape, 1)
        rest = jnp.where(lane // cap == row, gate, F32(0.0))
        for i in range(3):
            piece = rest.astype(BF)
            rest = rest - piece.astype(F32)
            got = jnp.dot(piece, m_ref[...], preferred_element_type=F32)
            refs[-1][i * experts : (i + 1) * experts, :] = got.astype(BF)

    return pl.pallas_call(
        kernel,
        in_specs=[pl.BlockSpec(memory_space=pltpu.VMEM)] * 2 + [HBM] * len(after),
        out_specs=pl.BlockSpec(memory_space=pltpu.VMEM),
        out_shape=jax.ShapeDtypeStruct((3 * experts, match.shape[1]), BF),
    )(returned, match, *after)


def shards(out_grad, router_weight, down_weight, hidden_saved, slot_token, slot_count, slot_gate):
    grad = out_grad[0]
    tokens = slot_token[0, 0]
    counts = slot_count[0, 0]
    gates = slot_gate[0, 0]
    weight = down_weight[0]
    held = hidden_saved[0, 0]
    experts, capacity = tokens.shape
    tok_count, width = grad.shape
    me = lax.axis_index("expert")
    mx, mz = me // NZ, me % NZ
    where = jnp.stack([mx, mz]).astype(jnp.int32)

    where = jnp.concatenate([jnp.stack([mx, mz]).astype(jnp.int32), counts])

    with jax.named_scope("next_section"):
        grad_next = passed_along(grad, "section", -1)
        router_next = passed_along(router_weight[0].T, "section", -1)
        router_next = jnp.concatenate([router_next] * 3, 0)

    def exchanged(rows):
        with jax.named_scope("exchange_x"):
            return [rows[0]] + [lax.ppermute(rows[k], "expert", shift_x(k)) for k in range(1, NX)]

    last = NZ // 2
    order = [[0]] + [[NZ - t, t] for t in range(1, last)] + [[last]]
    with jax.named_scope("pick"):
        own, rows = begin(where, grad, tokens, gates)
        near = [lax.ppermute(own, "expert", shift_z(k)) for k in (1, -1)]
    up = down = grad
    with jax.named_scope("exchange_x"):
        across = [[x * NZ + z for x in range(NX)] for z in range(NZ)]
        rows = lax.all_to_all(
            rows, "expert", split_axis=0, concat_axis=0, axis_index_groups=across, tiled=True
        )
    arrived, scaled, written = [[rows.reshape(-1, rows.shape[2])]], [], None
    for t in range(1, last + 1):
        with jax.named_scope("ring_z"):
            up = lax.ppermute(up, "expert", shift_z(1))
            down = lax.ppermute(down, "expert", shift_z(-1))
        with jax.named_scope("pick"):
            blocks = [[up], [down]] if t < last else [[up, down]]
            got = pick_rows(where, blocks, near if t == 1 else [], scaled[t - 2 : t - 1], t == last - 1)
            rows = got[:NX]
            if t < last:
                up, down = hold(got[NX:] or [up, down], arrived[t - 1][-3:] + [rows[0]])
            arrived.append(exchanged(rows))
        with jax.named_scope("project"):
            *written, piece = project(where, arrived[t - 1], weight, held, order[t - 1], written)
        scaled.append(piece)
    with jax.named_scope("project"):
        *written, piece = project(where, arrived[last], weight, held, order[last], written)
    scaled.append(piece)
    hidden_grad, partial = written

    with jax.named_scope("gate_return"):
        returned = lax.all_to_all(partial, "expert", split_axis=0, concat_axis=0, tiled=True)

    with jax.named_scope("weight_grad"):
        down_grad = weight_grad(where, [r for rows in arrived for r in rows], scaled, width)

    with jax.named_scope("input_grad"):
        slots = lax.broadcasted_iota(jnp.int32, (experts, capacity), 1)
        spot = jnp.where(slots < counts[:, None], tokens, -1).reshape(-1, 1)
        match = (spot == lax.broadcasted_iota(jnp.int32, (1, tok_count), 1)).astype(BF)
        logit_grad = logits(returned, match, [down_grad])
        logit_next = passed_along(logit_grad, "section", -1)
        passed = finish(where, grad_next, router_next, logit_next)
    return (down_grad[None], hidden_grad[None, None], passed[None])


def solution(mesh):
    return jax.shard_map(
        shards,
        mesh=mesh,
        in_specs=(
            P("section", "expert", None),
            P("section", None, None),
            P("section", "expert", None),
            P("section", "expert", None, None, None),
            P("section", "expert", None, None),
            P("section", "expert", None),
            P("section", "expert", None, None),
        ),
        out_specs=(
            P("section", "expert", None),
            P("section", "expert", None, None, None),
            P("section", "expert", None),
        ),
        check_vma=False,
    )
```
